1024 devices in a mesh: grp: 32 (over z), ep: 32 (over y, x, core).
Axes of the slice: x: 4, y: 4, z: 32, core: 2. Of those that a mesh axis runs over, the one named last changes fastest.
Arguments:
- tokens: bfloat16 [1024, 7168], P(('grp', 'ep')), may hold values from -6 to 6
- expert_ids: int32 [32, 32, 8], P('grp', 'ep'), may hold values from 0 to 31, all different within a row; in each aligned block of 32 rows (0 to 31, 32 to 63, ..., all dimensions but the last counted through in order) at most 8 rows name the same one
- affinity: bfloat16 [32, 32, 8], P('grp', 'ep'), may hold values from 0.3984375 to 1
- gate_up_blocks: bfloat16 [32, 32, 3584, 256], P('grp', 'ep'), may hold values from -0.0625 to 0.0625
- down_blocks: bfloat16 [32, 32, 128, 3584], P('grp', 'ep'), may hold values from -0.125 to 0.125
- queries: bfloat16 [1024, 128, 576], P(('grp', 'ep')), may hold values from -10 to 10
- latent_pool: bfloat16 [8192, 64, 576], P(('grp', 'ep')), may hold values from -6 to 6
- page_moves: int32 [1024, 4], P(('grp', 'ep')), may hold values from 0 to 7, as said below
- page_list: int32 [1024, 8], P(('grp', 'ep')), may hold values from 0 to 11, as said below
- lengths: int32 [1024], P(('grp', 'ep')), may hold values from 257 to 512, as said below
Outputs:
- attention_latent: bfloat16 [1024, 128, 512], P(('grp', 'ep'))
- expert_mix: bfloat16 [1024, 7168], P(('grp', 'ep'))
The draws below stay inside these ranges and needn't reach their ends.
Inputs may be any that keep to these rules, and one draw needn't show every extreme that they name: `expert_ids`: each token names 8 distinct experts; the 32 tokens of one grp index name every expert exactly 8 times. `page_moves`: distinct local page numbers in each row. `page_list`: distinct numbers in each row; page numbers 8 and above are the received pages (2 from below, then 2 from above), and they fill the first 4 entries in some order; the rest are local pages that the device does not hand over. `lengths`: every received page is read in full; some request reaches 512.
All inputs are finite; a program needn't handle non-finite values.
Results may differ from the reference program's by a relative error of at most 0.024.
Values may be sent and summed in bfloat16 or wider, within the bound.
No kernel may reach another device: no remote copies, remote signals or barrier semaphores. Data moves between devices by JAX's collectives and lax.ppermute only.
A program may use at most 64 MiB of HBM per device.

```python
import math
import jax
import jax.numpy as jnp
import numpy as np
from jax import lax

D = 7168
FF = 2048
HEADS = 128
KVL = 512
PAGE = 64
MSLOT = 2
PAGES = 8
LAT = 576
TOPK = 8
EXPERTS = 32
SPLIT = 16
UNITS = 128
CAP = 8
REQUESTS = 1024
N_GRP = 32
N_EP = 32


def page_orders(key):
    order_keys = jax.random.split(key, N_GRP * N_EP)
    return jax.vmap(lambda single: jax.random.permutation(single, PAGES))(order_keys).astype(jnp.int32)


def draw_queries(key, part):
    key = jax.random.fold_in(key, 31)
    array_shape = (N_GRP * N_EP, HEADS, LAT)
    values = jnp.clip(jax.random.normal(key, array_shape, jnp.float32), -6.0, 6.0)
    return values.astype(jnp.bfloat16)


def draw_latent_pool(key, part):
    key = jax.random.fold_in(key, 32)
    array_shape = (N_GRP * N_EP * PAGES, PAGE, LAT)
    values = jnp.clip(jax.random.normal(key, array_shape, jnp.float32), -6.0, 6.0)
    return values.astype(jnp.bfloat16)


def draw_page_moves(key, part):
    orders = page_orders(key)
    return orders[:, :2 * MSLOT]


def draw_page_list(key, part):
    orders = page_orders(key)
    key = jax.random.fold_in(key, 33)
    arrival_keys = jax.random.split(key, N_GRP * N_EP)
    arrivals = jax.vmap(lambda single: jax.random.permutation(single, 2 * MSLOT))(arrival_keys).astype(jnp.int32)
    return jnp.concatenate([arrivals + PAGES, orders[:, 2 * MSLOT:]], axis=1)


def draw_lengths(key, part):
    key = jax.random.fold_in(key, 34)
    drawn = jax.random.randint(key, (N_GRP * N_EP,), 2 * MSLOT * PAGE + 1, PAGES * PAGE + 1)
    return drawn.at[0].set(PAGES * PAGE).astype(jnp.int32)


def block_levels(stream_key, extent, cuts, smallest, largest):
    loudness, own = 1.0, jax.random.fold_in(stream_key, 6)
    for position, parts in cuts:
        steps = jnp.exp(jax.random.uniform(jax.random.fold_in(own, position), (parts,), jnp.float32, smallest / len(cuts), largest / len(cuts)))
        loudness = loudness * jnp.repeat(steps, extent[position] // parts).reshape([-1 if axis == position else 1 for axis in range(len(extent))])
    return loudness


def shared_out(rng, own, number, rows, amount, top, reach, lean):
    order = jax.random.permutation(rng, amount)
    packed, ordinary = portions_of(amount, rows * top, reach, lean, True), portions_of(amount, rows * top, reach, lean, False)
    places = jnp.arange(amount)

    def named(sizes, rotation):
        used = int((sizes > 0).sum())
        fixed = max(1, used // 4)
        shifted = fixed + (places - fixed + rotation * (used - fixed)) % max(1, amount - fixed)
        return jnp.zeros((amount,), jnp.int32).at[order[jnp.where(places < fixed, places, shifted)]].set(jnp.asarray(sizes, jnp.int32))

    sizes = jnp.where(number % 4 == 0, named(packed, number // 4), named(ordinary, number - number // 4 - 1))
    mixed = jax.random.permutation(jax.random.fold_in(own, 3), amount)
    source_of, taker = mixed[0:amount // 2 * 2:2], mixed[1:amount // 2 * 2:2]
    margin = jnp.minimum(sizes[source_of] - 1, reach - sizes[taker]) // 2
    margin = jnp.where((source_of == order[0]) | (taker == order[0]) | (sizes[taker] == 0), 0, jnp.maximum(margin, 0))
    shifted = jax.random.randint(jax.random.fold_in(own, 4), (amount // 2,), 0, 1 << 20) % (margin + 1)
    sizes = sizes.at[source_of].add(-shifted).at[taker].add(shifted)
    labels = jnp.searchsorted(jnp.cumsum(sizes), jnp.arange(rows * top), side="right").astype(jnp.int32)
    listing = labels.reshape(top, rows).T
    listing = listing[jax.random.permutation(jax.random.fold_in(own, 1), rows)]
    rotation = jax.random.randint(jax.random.fold_in(own, 2), (rows, 1), 0, top)
    return jnp.take_along_axis(listing, (jnp.arange(top)[None, :] + rotation) % top, axis=1)


def portions_of(number_of, total, most, skew, full):
    weights = [(1 << 20) // math.isqrt(rank ** skew) + 1 for rank in range(1, number_of + 1)]
    largest = most if full else min(most, max(-(-total // number_of), total * weights[0] // sum(weights)))
    least = 1 if total - largest >= number_of - 1 else 0
    given, rest = [largest] + [least] * (number_of - 1), total - largest - least * (number_of - 1)
    while rest > 0:
        candidates = [i for i in range(1, number_of) if given[i] < largest] or [i for i in range(1, number_of) if given[i] < most]
        pool, left = sum([weights[i] for i in candidates]), rest
        for i in candidates:
            addition = min(most - given[i], max(1, left * weights[i] // pool), rest)
            given[i] = given[i] + addition
            rest = rest - addition
    return np.array(given)


def normal_values(key, dims, spread, bound, pieces=(), kind=jnp.bfloat16):
    level = block_levels(key, dims, pieces, -0.22, 0.18) if pieces else 1.0
    result = jax.random.normal(key, dims, jnp.float32) * spread * level
    return jnp.minimum(jnp.maximum(result, -bound), bound).astype(kind)


def setup_inputs(seed: int = 0) -> dict:
    arg_keys = jax.random.split(jax.random.key(seed), 11)
    tokens = normal_values(arg_keys[0], (REQUESTS, D), 1.0, 6.0, ((0, 1024),))
    expert_ids_keys = jax.random.split(jax.random.fold_in(arg_keys[1], 1), N_GRP * N_EP // N_EP)
    expert_ids_turns = jax.random.permutation(jax.random.fold_in(arg_keys[1], 3), N_GRP * N_EP // N_EP)
    expert_ids = jax.vmap(lambda own, number: shared_out(jax.random.fold_in(arg_keys[1], 2), own, number, N_EP, EXPERTS, TOPK, CAP, 0))(expert_ids_keys, expert_ids_turns).reshape((N_GRP, N_EP, TOPK))
    affinity = jnp.clip(0.3984375 + 0.6015625 * jax.random.uniform(arg_keys[2], (N_GRP, N_EP, TOPK), jnp.float32) ** block_levels(arg_keys[2], (N_GRP, N_EP, TOPK), ((0, 32), (1, 32)), -0.2, 0.2), 0.3984375, 1.0).astype(jnp.bfloat16)
    gate_up_blocks = normal_values(arg_keys[3], (EXPERTS, N_EP, D // 2, 2 * UNITS), D ** -0.5, 0.0625, ((0, 32), (1, 32)))
    down_blocks = normal_values(arg_keys[4], (EXPERTS, N_EP, UNITS, D // 2), FF ** -0.5, 0.125, ((0, 32), (1, 32)))
    queries = draw_queries(jax.random.fold_in(arg_keys[10], 71), 0)
    latent_pool = draw_latent_pool(jax.random.fold_in(arg_keys[10], 71), 0)
    page_moves = draw_page_moves(jax.random.fold_in(arg_keys[10], 71), 0)
    page_list = draw_page_list(jax.random.fold_in(arg_keys[10], 71), 0)
    lengths = draw_lengths(jax.random.fold_in(arg_keys[10], 71), 0)
    return dict(tokens=tokens, expert_ids=expert_ids, affinity=affinity, gate_up_blocks=gate_up_blocks, down_blocks=down_blocks, queries=queries, latent_pool=latent_pool, page_moves=page_moves, page_list=page_list, lengths=lengths)


softmax_scale = 192.0 ** -0.5
routed_scale = 2.5


def attend(operands):
    extended, page_order, query_rows, length_now = operands
    latent_rows = jnp.take(extended, page_order, axis=0).reshape(PAGES * PAGE, LAT)
    scores = jnp.dot(query_rows, latent_rows.T, preferred_element_type=jnp.float32) * softmax_scale
    in_range = jnp.arange(PAGES * PAGE) < length_now
    scores = jnp.where(in_range[None, :], scores, -1e30)
    attention_weights = jax.nn.softmax(scores, axis=-1).astype(jnp.bfloat16)
    mixed_latent = jnp.dot(attention_weights, latent_rows[:, :KVL], preferred_element_type=jnp.float32)
    return mixed_latent.astype(jnp.bfloat16)


def reference(tokens, expert_ids, affinity, gate_up_blocks, down_blocks, queries, latent_pool, page_moves, page_list, lengths):
    request_count = N_GRP * N_EP
    pool_grid = latent_pool.reshape(N_GRP, N_EP, PAGES, PAGE, LAT)
    moves_grid = page_moves.reshape(N_GRP, N_EP, 2 * MSLOT)
    departing = jnp.take_along_axis(pool_grid, moves_grid[:, :, :, None, None], axis=2)
    from_lower = jnp.roll(departing[:, :, MSLOT:], 1, axis=1)
    from_upper = jnp.roll(departing[:, :, :MSLOT], -1, axis=1)
    extended = jnp.concatenate([pool_grid, from_lower, from_upper], axis=2)
    extended = extended.reshape(request_count, PAGES + 2 * MSLOT, PAGE, LAT)
    attention_latent = lax.map(attend, (extended, page_list, queries, lengths))

    chosen = expert_ids.reshape(request_count, TOPK)
    affinity_rows = affinity.reshape(request_count, TOPK).astype(jnp.float32)
    route_weights = routed_scale * affinity_rows / jnp.sum(affinity_rows, axis=1, keepdims=True)

    def per_expert(expert):
        matches = chosen == expert
        member = jnp.any(matches, axis=1).astype(jnp.int32)
        weight_of = jnp.sum(jnp.where(matches, route_weights, 0.0), axis=1)
        row_order = jnp.argsort(1 - member, stable=True)[: N_GRP * CAP].astype(jnp.int32)
        routed_rows = jnp.take(tokens, row_order, axis=0)
        blocks = gate_up_blocks[expert].reshape(2, SPLIT, D // 2, 2, UNITS)
        gate_matrix = blocks[:, :, :, 0, :].transpose(0, 2, 1, 3).reshape(D, FF)
        up_matrix = blocks[:, :, :, 1, :].transpose(0, 2, 1, 3).reshape(D, FF)
        gate_values = jnp.dot(routed_rows, gate_matrix, preferred_element_type=jnp.float32)
        up_values = jnp.dot(routed_rows, up_matrix, preferred_element_type=jnp.float32)
        activation = (jax.nn.silu(gate_values) * up_values).astype(jnp.bfloat16)
        down_matrix = down_blocks[expert].reshape(2, SPLIT, UNITS, D // 2).transpose(1, 2, 0, 3).reshape(SPLIT, UNITS, D)
        partial_out = jnp.einsum(
            "nsu,sud->nsd",
            activation.reshape(-1, SPLIT, UNITS).astype(jnp.float32),
            down_matrix.astype(jnp.float32),
            precision=lax.Precision.HIGHEST,
        ).astype(jnp.bfloat16)
        contribution = jnp.take(weight_of, row_order)[:, None] * jnp.sum(partial_out.astype(jnp.float32), axis=1)
        return row_order, contribution

    row_orders, contributions = lax.map(per_expert, jnp.arange(EXPERTS, dtype=jnp.int32))
    mixed = jnp.zeros((request_count, D), jnp.float32).at[row_orders.reshape(-1)].add(contributions.reshape(-1, D))
    return attention_latent, mixed.astype(jnp.bfloat16)
```

```python
import jax
import jax.numpy as jnp
from jax import lax
from jax.sharding import Mesh, PartitionSpec as P

KVL = 512
SLICE = 224
WIDE = 256
HALF = ("y", "x", "c")
EP = ("h",) + HALF


softmax_scale = 192.0 ** (-0.5)
routed_scale = 2.5


def exchanged(value, axes):
    return lax.all_to_all(value, axes, split_axis=0, concat_axis=0, tiled=True)


def attention_part(queries, latent_pool, page_moves, page_list, lengths):
    outgoing = page_moves.reshape(-1)
    moving = outgoing.shape[0] // 2
    departing = jnp.take(latent_pool, outgoing, axis=0)
    count = lax.axis_size(EP)
    forward = [(i, (i + 1) % count) for i in range(count)]
    backward = [(target, source) for source, target in forward]
    low = lax.ppermute(departing[moving:], EP, forward)
    high = lax.ppermute(departing[:moving], EP, backward)
    extended = jnp.concatenate([latent_pool, low, high], axis=0)
    latent_rows = jnp.take(extended, page_list.reshape(-1), axis=0)
    latent_rows = latent_rows.reshape(-1, latent_pool.shape[2])
    query_rows = queries.reshape(queries.shape[1], queries.shape[2])
    scores = jnp.dot(query_rows, latent_rows.T, preferred_element_type=jnp.float32) * softmax_scale
    in_range = jnp.arange(latent_rows.shape[0]) < lengths[0]
    scores = jnp.where(in_range[None, :], scores, -1e30)
    attention_weights = jax.nn.softmax(scores, axis=-1).astype(jnp.bfloat16)
    mixed_latent = jnp.dot(
        attention_weights, latent_rows[:, :KVL], preferred_element_type=jnp.float32
    )
    return mixed_latent.astype(jnp.bfloat16).reshape(1, query_rows.shape[0], KVL)


def expert_part(tokens, expert_ids, affinity, gate_up_blocks, down_blocks):
    members = lax.axis_size(EP)
    groups = lax.axis_size("z")
    parts = lax.axis_size(HALF)
    choices = expert_ids.shape[2]
    capacity = members * choices // groups
    gate_up = gate_up_blocks.reshape(parts, SLICE, gate_up_blocks.shape[3])
    units = gate_up.shape[2] // 2
    down = down_blocks.reshape(units, parts, SLICE)
    down = jnp.pad(down.transpose(1, 0, 2), ((0, 0), (0, 0), (0, WIDE - SLICE)))
    routing = jnp.concatenate(
        [expert_ids.reshape(1, choices).astype(jnp.bfloat16), affinity.reshape(1, choices)], axis=1
    )
    routing = jnp.pad(routing, ((0, 0), (0, WIDE - SLICE - 2 * choices)))
    outgoing = jnp.concatenate(
        [tokens.reshape(members, SLICE), jnp.broadcast_to(routing, (members, WIDE - SLICE))], axis=1
    )
    held = exchanged(outgoing, EP)
    chosen = held[:, SLICE : SLICE + choices].astype(jnp.float32)
    affinity_all = held[:, SLICE + choices : SLICE + 2 * choices].astype(jnp.float32)
    route_weights = routed_scale * affinity_all / jnp.sum(affinity_all, axis=1, keepdims=True)
    matches = chosen[:, :, None] == jnp.arange(groups, dtype=jnp.float32)[None, None, :]
    member = jnp.any(matches, axis=1)
    weight_of = jnp.sum(jnp.where(matches, route_weights[:, :, None], 0.0), axis=1)
    earlier = jnp.arange(members)[:, None] > jnp.arange(members)[None, :]
    position = jnp.dot(
        earlier.astype(jnp.bfloat16),
        member.astype(jnp.bfloat16),
        preferred_element_type=jnp.float32,
    )
    slot_number = jnp.arange(capacity, dtype=jnp.float32)
    selector = member.T[:, None, :] & (position.T[:, None, :] == slot_number[None, :, None])
    rows = groups * capacity
    sent_rows = jnp.dot(
        selector.astype(jnp.bfloat16).reshape(rows, members),
        held,
        preferred_element_type=jnp.float32,
    ).astype(jnp.bfloat16)
    arrived = exchanged(sent_rows.reshape(groups, capacity, WIDE), "z").reshape(rows, WIDE)
    gathered = lax.all_gather(arrived, HALF, axis=0, tiled=False)
    partial_sum = jnp.einsum(
        "urk,ukn->rn", gathered[:, :, :SLICE], gate_up, preferred_element_type=jnp.float32
    )
    partner_sum = lax.ppermute(partial_sum.astype(jnp.bfloat16), "h", [(0, 1), (1, 0)])
    combined = partial_sum + partner_sum.astype(jnp.float32)
    activation = (jax.nn.silu(combined[:, :units]) * combined[:, units:]).astype(jnp.bfloat16)
    partial_out = jnp.einsum(
        "ru,cuk->crk", activation, down, preferred_element_type=jnp.float32
    ).astype(jnp.bfloat16)
    summed = jnp.sum(exchanged(partial_out, HALF).astype(jnp.float32), axis=0)
    summed = summed.astype(jnp.bfloat16).reshape(groups, capacity, WIDE)
    returned = exchanged(summed, "z").reshape(rows, WIDE)
    weighted = jnp.where(selector, weight_of.T[:, None, :], 0.0).reshape(rows, members)
    mixed = jnp.einsum(
        "rn,rk->nk", weighted, returned.astype(jnp.float32), precision=lax.Precision.HIGHEST
    )
    own = exchanged(mixed.astype(jnp.bfloat16), EP)
    return own[:, :SLICE].reshape(1, -1)


def shards(
    tokens,
    expert_ids,
    affinity,
    gate_up_blocks,
    down_blocks,
    queries,
    latent_pool,
    page_moves,
    page_list,
    lengths,
):
    attention_latent = attention_part(queries, latent_pool, page_moves, page_list, lengths)
    expert_mix = expert_part(tokens, expert_ids, affinity, gate_up_blocks, down_blocks)
    return (attention_latent, expert_mix)


def solution(mesh):
    fine = Mesh(mesh.devices.reshape(32, 2, 2, 4, 2), ("z",) + EP)
    both = ("z",) + EP
    placed = (
        P(both, None),
        P("z", EP, None),
        P("z", EP, None),
        P("z", EP, None, None),
        P("z", EP, None, None),
        P(both, None, None),
        P(both, None, None),
        P(both, None),
        P(both, None),
        P(both),
    )
    return jax.shard_map(
        shards,
        mesh=fine,
        in_specs=placed,
        out_specs=(P(both, None, None), P(both, None)),
        check_vma=False,
    )
```

```python
import jax
import jax.numpy as jnp
from jax import lax
from jax.sharding import Mesh, PartitionSpec as P

KVL = 512
SLICE = 224
WIDE = 256
HALF = ("y", "x", "c")
EP = ("h",) + HALF


softmax_scale = 192.0 ** (-0.5)
routed_scale = 2.5


def exchanged(value, axes):
    return lax.all_to_all(value, axes, split_axis=0, concat_axis=0, tiled=True)


def attention_part(queries, latent_pool, page_moves, page_list, lengths):
    outgoing = page_moves.reshape(-1)
    moving = outgoing.shape[0] // 2
    departing = jnp.take(latent_pool, outgoing, axis=0)
    count = lax.axis_size(EP)
    forward = [(i, (i + 1) % count) for i in range(count)]
    backward = [(target, source) for source, target in forward]
    low = lax.ppermute(departing[moving:], EP, forward)
    high = lax.ppermute(departing[:moving], EP, backward)
    extended = jnp.concatenate([latent_pool, low, high], axis=0)
    latent_rows = jnp.take(extended, page_list.reshape(-1), axis=0)
    latent_rows = latent_rows.reshape(-1, latent_pool.shape[2])
    query_rows = queries.reshape(queries.shape[1], queries.shape[2])
    scores = jnp.dot(query_rows, latent_rows.T, preferred_element_type=jnp.float32) * softmax_scale
    in_range = jnp.arange(latent_rows.shape[0]) < lengths[0]
    scores = jnp.where(in_range[None, :], scores, -1e30)
    attention_weights = jax.nn.softmax(scores, axis=-1).astype(jnp.bfloat16)
    mixed_latent = jnp.dot(
        attention_weights, latent_rows[:, :KVL], preferred_element_type=jnp.float32
    )
    return mixed_latent.astype(jnp.bfloat16).reshape(1, query_rows.shape[0], KVL)


def expert_part(tokens, expert_ids, affinity, gate_up_blocks, down_blocks):
    members = lax.axis_size(EP)
    groups = lax.axis_size("z")
    parts = lax.axis_size(HALF)
    choices = expert_ids.shape[2]
    capacity = members * choices // groups
    gate_up = gate_up_blocks.reshape(parts, SLICE, gate_up_blocks.shape[3])
    units = gate_up.shape[2] // 2
    down = down_blocks.reshape(units, parts, SLICE)
    down = jnp.pad(down.transpose(1, 0, 2), ((0, 0), (0, 0), (0, WIDE - SLICE)))
    routing = jnp.concatenate(
        [expert_ids.reshape(1, choices).astype(jnp.bfloat16), affinity.reshape(1, choices)], axis=1
    )
    routing = jnp.pad(routing, ((0, 0), (0, WIDE - SLICE - 2 * choices)))
    outgoing = jnp.concatenate(
        [tokens.reshape(members, SLICE), jnp.broadcast_to(routing, (members, WIDE - SLICE))], axis=1
    )
    held = exchanged(outgoing, EP)
    chosen = held[:, SLICE : SLICE + choices].astype(jnp.float32)
    affinity_all = held[:, SLICE + choices : SLICE + 2 * choices].astype(jnp.float32)
    route_weights = routed_scale * affinity_all / jnp.sum(affinity_all, axis=1, keepdims=True)
    matches = chosen[:, :, None] == jnp.arange(groups, dtype=jnp.float32)[None, None, :]
    member = jnp.any(matches, axis=1)
    weight_of = jnp.sum(jnp.where(matches, route_weights[:, :, None], 0.0), axis=1)
    earlier = jnp.arange(members)[:, None] > jnp.arange(members)[None, :]
    position = jnp.dot(
        earlier.astype(jnp.bfloat16),
        member.astype(jnp.bfloat16),
        preferred_element_type=jnp.float32,
    )
    slot_number = jnp.arange(capacity, dtype=jnp.float32)
    selector = member.T[:, None, :] & (position.T[:, None, :] == slot_number[None, :, None])
    rows = groups * capacity
    sent_rows = jnp.dot(
        selector.astype(jnp.bfloat16).reshape(rows, members),
        held,
        preferred_element_type=jnp.float32,
    ).astype(jnp.bfloat16)
    arrived = exchanged(sent_rows.reshape(groups, capacity, WIDE), "z").reshape(rows, WIDE)
    chips = parts // 2
    same_core = exchanged(jnp.broadcast_to(arrived[None], (chips, rows, WIDE)), ("y", "x"))
    other_core = lax.ppermute(same_core, "c", [(0, 1), (1, 0)])
    by_core = gate_up.reshape(chips, 2, SLICE, 2 * units)
    core = lax.axis_index("c")
    same_weights = lax.dynamic_index_in_dim(by_core, core, 1, keepdims=False)
    other_weights = lax.dynamic_index_in_dim(by_core, 1 - core, 1, keepdims=False)
    partial_sum = jnp.einsum(
        "urk,ukn->rn", same_core[:, :, :SLICE], same_weights, preferred_element_type=jnp.float32
    ) + jnp.einsum(
        "urk,ukn->rn", other_core[:, :, :SLICE], other_weights, preferred_element_type=jnp.float32
    )
    partner_sum = lax.ppermute(partial_sum.astype(jnp.bfloat16), "h", [(0, 1), (1, 0)])
    combined = partial_sum + partner_sum.astype(jnp.float32)
    activation = (jax.nn.silu(combined[:, :units]) * combined[:, units:]).astype(jnp.bfloat16)
    partial_out = jnp.einsum(
        "ru,cuk->crk", activation, down, preferred_element_type=jnp.float32
    ).astype(jnp.bfloat16)
    summed = jnp.sum(exchanged(partial_out, HALF).astype(jnp.float32), axis=0)
    summed = summed.astype(jnp.bfloat16).reshape(groups, capacity, WIDE)
    returned = exchanged(summed, "z").reshape(rows, WIDE)
    weighted = jnp.where(selector, weight_of.T[:, None, :], 0.0).reshape(rows, members)
    mixed = jnp.einsum(
        "rn,rk->nk", weighted, returned.astype(jnp.float32), precision=lax.Precision.HIGHEST
    )
    own = exchanged(mixed.astype(jnp.bfloat16), EP)
    return own[:, :SLICE].reshape(1, -1)


def shards(
    tokens,
    expert_ids,
    affinity,
    gate_up_blocks,
    down_blocks,
    queries,
    latent_pool,
    page_moves,
    page_list,
    lengths,
):
    attention_latent = attention_part(queries, latent_pool, page_moves, page_list, lengths)
    expert_mix = expert_part(tokens, expert_ids, affinity, gate_up_blocks, down_blocks)
    return (attention_latent, expert_mix)


def solution(mesh):
    fine = Mesh(mesh.devices.reshape(32, 2, 2, 4, 2), ("z",) + EP)
    both = ("z",) + EP
    placed = (
        P(both, None),
        P("z", EP, None),
        P("z", EP, None),
        P("z", EP, None, None),
        P("z", EP, None, None),
        P(both, None, None),
        P(both, None, None),
        P(both, None),
        P(both, None),
        P(both),
    )
    return jax.shard_map(
        shards,
        mesh=fine,
        in_specs=placed,
        out_specs=(P(both, None, None), P(both, None)),
        check_vma=False,
    )
```

```python
import jax
import jax.numpy as jnp
from jax import lax
from jax.experimental import pallas as pl
from jax.experimental.pallas import tpu as pltpu
from jax.sharding import Mesh, PartitionSpec as P

KVL = 512
SLICE = 224
WIDE = 256
HALF = ("y", "x", "c")
CHIPS = ("h", "y", "x")
EP = ("h",) + HALF


softmax_scale = 192.0 ** (-0.5)
routed_scale = 2.5


def exchanged(value, axes):
    return lax.all_to_all(value, axes, split_axis=0, concat_axis=0, tiled=True)


def gate_up_kernel(core, own, other, weights, out):
    mine = core[0]
    chips, units = weights.shape[0], weights.shape[3] // 2
    part = units // 2
    for i in range(chips):
        sums = jnp.dot(own[...], weights[i, mine], preferred_element_type=jnp.float32)
        sums += jnp.dot(other[...], weights[i, 1 - mine], preferred_element_type=jnp.float32)
        for h in range(2):
            pair = [sums[:, n * part : (n + 1) * part] for n in (h, 2 + h)]
            out[h * chips + i] = jnp.concatenate(pair, axis=1).astype(out.dtype)


def gate_up_sums(core, own, other, weights):
    chips, _, width, columns = weights.shape
    rows = own.shape[0]
    out_shape = (2 * chips, rows, columns // 2)
    return pl.pallas_call(
        gate_up_kernel,
        out_shape=jax.ShapeDtypeStruct(out_shape, jnp.bfloat16),
        in_specs=[pl.BlockSpec(memory_space=pltpu.SMEM)]
        + [pl.BlockSpec(memory_space=pltpu.VMEM)] * 3,
        out_specs=pl.BlockSpec(memory_space=pltpu.VMEM),
        compiler_params=pltpu.CompilerParams(vmem_limit_bytes=32 << 20),
        cost_estimate=pl.CostEstimate(
            flops=4 * chips * rows * width * columns,
            bytes_accessed=2 * weights.size + 4 * out_shape[0] * rows * columns // 2,
            transcendentals=0,
        ),
    )(core, own, other, weights)


def activation_kernel(parts, out):
    units = parts.shape[2] // 2
    sums = parts[0].astype(jnp.float32)
    for n in range(1, parts.shape[0]):
        sums += parts[n].astype(jnp.float32)
    gate, up = sums[:, :units], sums[:, units:]
    value = (jax.nn.silu(gate) * up).T.astype(out.dtype)
    for n in range(out.shape[0]):
        out[n] = value


def activated(parts):
    count, rows, columns = parts.shape
    out_shape = (count, columns // 2, rows)
    return pl.pallas_call(
        activation_kernel,
        out_shape=jax.ShapeDtypeStruct(out_shape, jnp.bfloat16),
        in_specs=[pl.BlockSpec(memory_space=pltpu.VMEM)],
        out_specs=pl.BlockSpec(memory_space=pltpu.VMEM),
        compiler_params=pltpu.CompilerParams(vmem_limit_bytes=32 << 20),
        cost_estimate=pl.CostEstimate(
            flops=2 * parts.size, bytes_accessed=3 * parts.size, transcendentals=0
        ),
    )(parts)


def down_kernel(core, values, weights, kept, given):
    mine = core[0]
    chips, _, units, width = weights.shape
    pieces = [values[h * chips + i] for i in range(chips) for h in range(2)]
    held = jnp.concatenate(pieces, axis=0)
    for n, out in ((mine, kept), (1 - mine, given)):
        matrix = jnp.concatenate([weights[i, n] for i in range(chips)], axis=0)
        out[...] = lax.dot_general(
            held, matrix, (((0,), (0,)), ((), ())), preferred_element_type=jnp.float32
        ).astype(out.dtype)


def down_sums(core, values, weights):
    chips, _, units, width = weights.shape
    rows = values.shape[2]
    return pl.pallas_call(
        down_kernel,
        out_shape=(
            jax.ShapeDtypeStruct((rows, width), jnp.float32),
            jax.ShapeDtypeStruct((rows, width), jnp.bfloat16),
        ),
        in_specs=[pl.BlockSpec(memory_space=pltpu.SMEM)]
        + [pl.BlockSpec(memory_space=pltpu.VMEM)] * 2,
        out_specs=(pl.BlockSpec(memory_space=pltpu.VMEM),) * 2,
        compiler_params=pltpu.CompilerParams(vmem_limit_bytes=32 << 20),
        cost_estimate=pl.CostEstimate(
            flops=4 * chips * rows * width * units,
            bytes_accessed=2 * weights.size + 2 * values.size + 6 * rows * width,
            transcendentals=0,
        ),
    )(core, values, weights)


def attention_part(queries, latent_pool, page_moves, page_list, lengths):
    outgoing = page_moves.reshape(-1)
    moving = outgoing.shape[0] // 2
    departing = jnp.take(latent_pool, outgoing, axis=0)
    count = lax.axis_size(EP)
    forward = [(i, (i + 1) % count) for i in range(count)]
    backward = [(target, source) for source, target in forward]
    low = lax.ppermute(departing[moving:], EP, forward)
    high = lax.ppermute(departing[:moving], EP, backward)
    extended = jnp.concatenate([latent_pool, low, high], axis=0)
    latent_rows = jnp.take(extended, page_list.reshape(-1), axis=0)
    latent_rows = latent_rows.reshape(-1, latent_pool.shape[2])
    query_rows = queries.reshape(queries.shape[1], queries.shape[2])
    scores = jnp.dot(query_rows, latent_rows.T, preferred_element_type=jnp.float32) * softmax_scale
    in_range = jnp.arange(latent_rows.shape[0]) < lengths[0]
    scores = jnp.where(in_range[None, :], scores, -1e30)
    attention_weights = jax.nn.softmax(scores, axis=-1).astype(jnp.bfloat16)
    mixed_latent = jnp.dot(
        attention_weights, latent_rows[:, :KVL], preferred_element_type=jnp.float32
    )
    return mixed_latent.astype(jnp.bfloat16).reshape(1, query_rows.shape[0], KVL)


def expert_part(tokens, expert_ids, affinity, gate_up_blocks, down_blocks):
    members = lax.axis_size(EP)
    groups = lax.axis_size("z")
    parts = lax.axis_size(HALF)
    choices = expert_ids.shape[2]
    capacity = members * choices // groups
    chips = parts // 2
    units = gate_up_blocks.shape[3] // 2
    routing = jnp.concatenate(
        [expert_ids.reshape(1, choices).astype(jnp.bfloat16), affinity.reshape(1, choices)], axis=1
    )
    routing = jnp.pad(routing, ((0, 0), (0, WIDE - SLICE - 2 * choices)))
    outgoing = jnp.concatenate(
        [tokens.reshape(members, SLICE), jnp.broadcast_to(routing, (members, WIDE - SLICE))], axis=1
    )
    held = exchanged(outgoing, EP)
    chosen = held[:, SLICE : SLICE + choices].astype(jnp.float32)
    affinity_all = held[:, SLICE + choices : SLICE + 2 * choices].astype(jnp.float32)
    route_weights = routed_scale * affinity_all / jnp.sum(affinity_all, axis=1, keepdims=True)
    matches = chosen[:, :, None] == jnp.arange(groups, dtype=jnp.float32)[None, None, :]
    member = jnp.any(matches, axis=1)
    weight_of = jnp.sum(jnp.where(matches, route_weights[:, :, None], 0.0), axis=1)
    earlier = jnp.arange(members)[:, None] > jnp.arange(members)[None, :]
    position = jnp.dot(
        earlier.astype(jnp.bfloat16),
        member.astype(jnp.bfloat16),
        preferred_element_type=jnp.float32,
    )
    slot_number = jnp.arange(capacity, dtype=jnp.float32)
    selector = member.T[:, None, :] & (position.T[:, None, :] == slot_number[None, :, None])
    rows = groups * capacity
    sent_rows = jnp.dot(
        selector.astype(jnp.bfloat16).reshape(rows, members),
        held[:, :SLICE],
        preferred_element_type=jnp.float32,
    ).astype(jnp.bfloat16)
    arrived = exchanged(sent_rows.reshape(groups, capacity, SLICE), "z").reshape(rows, SLICE)
    gate_up = gate_up_blocks.reshape(chips, 2 * SLICE, 2 * units)
    gate_up = exchanged(gate_up, ("y", "x")).reshape(chips, 2, SLICE, 2 * units)
    down = down_blocks.reshape(units, chips, 2, SLICE).transpose(1, 2, 0, 3)
    down = exchanged(down, ("y", "x"))
    core = lax.axis_index("c").reshape(1).astype(jnp.int32)
    other = lax.ppermute(arrived, "c", [(0, 1), (1, 0)])
    partial_sum = gate_up_sums(core, arrived, other, gate_up)
    activation = activated(exchanged(partial_sum, CHIPS))
    activation = exchanged(activation, CHIPS)
    kept, given = down_sums(core, activation, down)
    summed = kept + lax.ppermute(given, "c", [(0, 1), (1, 0)]).astype(jnp.float32)
    summed = summed.astype(jnp.bfloat16).reshape(groups, capacity, SLICE)
    returned = exchanged(summed, "z").reshape(rows, SLICE)
    weighted = jnp.where(selector, weight_of.T[:, None, :], 0.0).reshape(rows, members)
    mixed = jnp.einsum(
        "rn,rk->nk", weighted, returned.astype(jnp.float32), precision=lax.Precision.HIGHEST
    )
    return exchanged(mixed.astype(jnp.bfloat16), EP).reshape(1, -1)


def shards(
    tokens,
    expert_ids,
    affinity,
    gate_up_blocks,
    down_blocks,
    queries,
    latent_pool,
    page_moves,
    page_list,
    lengths,
):
    attention_latent = attention_part(queries, latent_pool, page_moves, page_list, lengths)
    expert_mix = expert_part(tokens, expert_ids, affinity, gate_up_blocks, down_blocks)
    return (attention_latent, expert_mix)


def solution(mesh):
    fine = Mesh(mesh.devices.reshape(32, 2, 2, 4, 2), ("z",) + EP)
    both = ("z",) + EP
    placed = (
        P(both, None),
        P("z", EP, None),
        P("z", EP, None),
        P("z", EP, None, None),
        P("z", EP, None, None),
        P(both, None, None),
        P(both, None, None),
        P(both, None),
        P(both, None),
        P(both),
    )
    return jax.shard_map(
        shards,
        mesh=fine,
        in_specs=placed,
        out_specs=(P(both, None, None), P(both, None)),
        check_vma=False,
    )
```

```python
import jax
import jax.numpy as jnp
from jax import lax
from jax.experimental import pallas as pl
from jax.experimental.pallas import tpu as pltpu
from jax.sharding import Mesh, PartitionSpec as P

KVL = 512
SLICE = 224
WIDE = 256
HALF = ("y", "x", "c")
EP = ("h",) + HALF


softmax_scale = 192.0 ** (-0.5)
routed_scale = 2.5


def exchanged(value, axes):
    return lax.all_to_all(value, axes, split_axis=0, concat_axis=0, tiled=True)


def activation_kernel(own, partner, out):
    units = out.shape[1]
    sums = own[...] + partner[...].astype(jnp.float32)
    gate, up = sums[:, :units], sums[:, units:]
    value = (jax.nn.silu(gate) * up).T.astype(out.dtype)
    for n in range(out.shape[0]):
        out[n] = value


def activated(own, partner, count):
    rows, columns = own.shape
    out_shape = (count, columns // 2, rows)
    return pl.pallas_call(
        activation_kernel,
        out_shape=jax.ShapeDtypeStruct(out_shape, jnp.bfloat16),
        in_specs=[pl.BlockSpec(memory_space=pltpu.VMEM)] * 2,
        out_specs=pl.BlockSpec(memory_space=pltpu.VMEM),
        compiler_params=pltpu.CompilerParams(vmem_limit_bytes=32 << 20),
        cost_estimate=pl.CostEstimate(
            flops=8 * own.size, bytes_accessed=6 * own.size + count * own.size, transcendentals=0
        ),
    )(own, partner)


def down_kernel(core, values, weights, kept, given):
    mine = core[0]
    chips, _, units, width = weights.shape
    held = jnp.concatenate([values[i] for i in range(chips)], axis=0)
    for n, out in ((mine, kept), (1 - mine, given)):
        matrix = jnp.concatenate([weights[i, n] for i in range(chips)], axis=0)
        out[...] = lax.dot_general(
            held, matrix, (((0,), (0,)), ((), ())), preferred_element_type=jnp.float32
        ).astype(out.dtype)


def down_sums(core, values, weights):
    chips, _, units, width = weights.shape
    rows = values.shape[2]
    return pl.pallas_call(
        down_kernel,
        out_shape=(
            jax.ShapeDtypeStruct((rows, width), jnp.float32),
            jax.ShapeDtypeStruct((rows, width), jnp.bfloat16),
        ),
        in_specs=[pl.BlockSpec(memory_space=pltpu.SMEM)]
        + [pl.BlockSpec(memory_space=pltpu.VMEM)] * 2,
        out_specs=(pl.BlockSpec(memory_space=pltpu.VMEM),) * 2,
        compiler_params=pltpu.CompilerParams(vmem_limit_bytes=32 << 20),
        cost_estimate=pl.CostEstimate(
            flops=4 * chips * rows * width * units,
            bytes_accessed=2 * weights.size + 2 * values.size + 6 * rows * width,
            transcendentals=0,
        ),
    )(core, values, weights)


def attention_part(queries, latent_pool, page_moves, page_list, lengths):
    outgoing = page_moves.reshape(-1)
    moving = outgoing.shape[0] // 2
    departing = jnp.take(latent_pool, outgoing, axis=0)
    count = lax.axis_size(EP)
    forward = [(i, (i + 1) % count) for i in range(count)]
    backward = [(target, source) for source, target in forward]
    low = lax.ppermute(departing[moving:], EP, forward)
    high = lax.ppermute(departing[:moving], EP, backward)
    extended = jnp.concatenate([latent_pool, low, high], axis=0)
    latent_rows = jnp.take(extended, page_list.reshape(-1), axis=0)
    latent_rows = latent_rows.reshape(-1, latent_pool.shape[2])
    query_rows = queries.reshape(queries.shape[1], queries.shape[2])
    scores = jnp.dot(query_rows, latent_rows.T, preferred_element_type=jnp.float32) * softmax_scale
    in_range = jnp.arange(latent_rows.shape[0]) < lengths[0]
    scores = jnp.where(in_range[None, :], scores, -1e30)
    attention_weights = jax.nn.softmax(scores, axis=-1).astype(jnp.bfloat16)
    mixed_latent = jnp.dot(
        attention_weights, latent_rows[:, :KVL], preferred_element_type=jnp.float32
    )
    return mixed_latent.astype(jnp.bfloat16).reshape(1, query_rows.shape[0], KVL)


def expert_part(tokens, expert_ids, affinity, gate_up_blocks, down_blocks):
    members = lax.axis_size(EP)
    groups = lax.axis_size("z")
    parts = lax.axis_size(HALF)
    choices = expert_ids.shape[2]
    capacity = members * choices // groups
    chips = parts // 2
    units = gate_up_blocks.shape[3] // 2
    routing = jnp.concatenate(
        [expert_ids.reshape(1, choices).astype(jnp.bfloat16), affinity.reshape(1, choices)], axis=1
    )
    routing = jnp.pad(routing, ((0, 0), (0, WIDE - SLICE - 2 * choices)))
    outgoing = jnp.concatenate(
        [tokens.reshape(members, SLICE), jnp.broadcast_to(routing, (members, WIDE - SLICE))], axis=1
    )
    held = exchanged(outgoing, EP)
    chosen = held[:, SLICE : SLICE + choices].astype(jnp.float32)
    affinity_all = held[:, SLICE + choices : SLICE + 2 * choices].astype(jnp.float32)
    route_weights = routed_scale * affinity_all / jnp.sum(affinity_all, axis=1, keepdims=True)
    matches = chosen[:, :, None] == jnp.arange(groups, dtype=jnp.float32)[None, None, :]
    member = jnp.any(matches, axis=1)
    weight_of = jnp.sum(jnp.where(matches, route_weights[:, :, None], 0.0), axis=1)
    earlier = jnp.arange(members)[:, None] > jnp.arange(members)[None, :]
    position = jnp.dot(
        earlier.astype(jnp.bfloat16),
        member.astype(jnp.bfloat16),
        preferred_element_type=jnp.float32,
    )
    slot_number = jnp.arange(capacity, dtype=jnp.float32)
    selector = member.T[:, None, :] & (position.T[:, None, :] == slot_number[None, :, None])
    rows = groups * capacity
    sent_rows = jnp.dot(
        selector.astype(jnp.bfloat16).reshape(rows, members),
        held[:, :SLICE],
        preferred_element_type=jnp.float32,
    ).astype(jnp.bfloat16)
    arrived = exchanged(sent_rows.reshape(groups, capacity, SLICE), "z").reshape(rows, SLICE)
    same_core = exchanged(jnp.broadcast_to(arrived[None], (chips, rows, SLICE)), ("y", "x"))
    down = down_blocks.reshape(units, chips, 2, SLICE).transpose(1, 2, 0, 3)
    down, same_core = lax.optimization_barrier((down, same_core))
    down = exchanged(down, ("y", "x"))
    other_core = lax.ppermute(same_core, "c", [(0, 1), (1, 0)])
    by_core = gate_up_blocks.reshape(chips, 2, SLICE, 2 * units)
    core = lax.axis_index("c")
    same_weights = lax.dynamic_index_in_dim(by_core, core, 1, keepdims=False)
    other_weights = lax.dynamic_index_in_dim(by_core, 1 - core, 1, keepdims=False)
    partial_sum = jnp.einsum(
        "urk,ukn->rn", same_core, same_weights, preferred_element_type=jnp.float32
    ) + jnp.einsum("urk,ukn->rn", other_core, other_weights, preferred_element_type=jnp.float32)
    partner_sum = lax.ppermute(partial_sum.astype(jnp.bfloat16), "h", [(0, 1), (1, 0)])
    activation = activated(partial_sum, partner_sum, chips)
    activation, down = lax.optimization_barrier((activation, down))
    activation = exchanged(activation, ("y", "x"))
    core = core.reshape(1).astype(jnp.int32)
    kept, given = down_sums(core, activation, down)
    summed = kept + lax.ppermute(given, "c", [(0, 1), (1, 0)]).astype(jnp.float32)
    summed = summed.astype(jnp.bfloat16).reshape(groups, capacity, SLICE)
    returned = exchanged(summed, "z").reshape(rows, SLICE)
    weighted = jnp.where(selector, weight_of.T[:, None, :], 0.0).reshape(rows, members)
    mixed = jnp.einsum(
        "rn,rk->nk", weighted, returned.astype(jnp.float32), precision=lax.Precision.HIGHEST
    )
    return exchanged(mixed.astype(jnp.bfloat16), EP).reshape(1, -1)


def shards(
    tokens,
    expert_ids,
    affinity,
    gate_up_blocks,
    down_blocks,
    queries,
    latent_pool,
    page_moves,
    page_list,
    lengths,
):
    attention_latent = attention_part(queries, latent_pool, page_moves, page_list, lengths)
    expert_mix = expert_part(tokens, expert_ids, affinity, gate_up_blocks, down_blocks)
    return (attention_latent, expert_mix)


def solution(mesh):
    fine = Mesh(mesh.devices.reshape(32, 2, 2, 4, 2), ("z",) + EP)
    both = ("z",) + EP
    placed = (
        P(both, None),
        P("z", EP, None),
        P("z", EP, None),
        P("z", EP, None, None),
        P("z", EP, None, None),
        P(both, None, None),
        P(both, None, None),
        P(both, None),
        P(both, None),
        P(both),
    )
    return jax.shard_map(
        shards,
        mesh=fine,
        in_specs=placed,
        out_specs=(P(both, None, None), P(both, None)),
        check_vma=False,
    )
```

```python
import jax
import jax.numpy as jnp
from jax import lax
from jax.experimental import pallas as pl
from jax.experimental.pallas import tpu as pltpu
from jax.sharding import Mesh, PartitionSpec as P

KVL = 512
SLICE = 224
WIDE = 256
HALF = ("y", "x", "c")
EP = ("h",) + HALF


softmax_scale = 192.0 ** (-0.5)
routed_scale = 2.5


def exchanged(value, axes):
    return lax.all_to_all(value, axes, split_axis=0, concat_axis=0, tiled=True)


def activation_kernel(own, partner, out):
    units = out.shape[1]
    sums = own[...] + partner[...].astype(jnp.float32)
    gate, up = sums[:, :units], sums[:, units:]
    value = (jax.nn.silu(gate) * up).T.astype(out.dtype)
    for n in range(out.shape[0]):
        out[n] = value


def activated(own, partner, count):
    rows, columns = own.shape
    out_shape = (count, columns // 2, rows)
    return pl.pallas_call(
        activation_kernel,
        out_shape=jax.ShapeDtypeStruct(out_shape, jnp.bfloat16),
        in_specs=[pl.BlockSpec(memory_space=pltpu.VMEM)] * 2,
        out_specs=pl.BlockSpec(memory_space=pltpu.VMEM),
        compiler_params=pltpu.CompilerParams(vmem_limit_bytes=32 << 20),
        cost_estimate=pl.CostEstimate(
            flops=8 * own.size, bytes_accessed=6 * own.size + count * own.size, transcendentals=0
        ),
    )(own, partner)


def down_kernel(core, values, weights, kept, given):
    mine = core[0]
    chips, _, units, width = weights.shape
    held = jnp.concatenate([values[i] for i in range(chips)], axis=0)
    for n, out in ((mine, kept), (1 - mine, given)):
        matrix = jnp.concatenate([weights[i, n] for i in range(chips)], axis=0)
        out[...] = lax.dot_general(
            held, matrix, (((0,), (0,)), ((), ())), preferred_element_type=jnp.float32
        ).astype(out.dtype)


def down_sums(core, values, weights):
    chips, _, units, width = weights.shape
    rows = values.shape[2]
    return pl.pallas_call(
        down_kernel,
        out_shape=(
            jax.ShapeDtypeStruct((rows, width), jnp.float32),
            jax.ShapeDtypeStruct((rows, width), jnp.bfloat16),
        ),
        in_specs=[pl.BlockSpec(memory_space=pltpu.SMEM)]
        + [pl.BlockSpec(memory_space=pltpu.VMEM)] * 2,
        out_specs=(pl.BlockSpec(memory_space=pltpu.VMEM),) * 2,
        compiler_params=pltpu.CompilerParams(vmem_limit_bytes=32 << 20),
        cost_estimate=pl.CostEstimate(
            flops=4 * chips * rows * width * units,
            bytes_accessed=2 * weights.size + 2 * values.size + 6 * rows * width,
            transcendentals=0,
        ),
    )(core, values, weights)


def whole(count):
    return [pl.BlockSpec(memory_space=pltpu.VMEM)] * count


def page_kernel(moves, first, rest, lower, higher):
    lower[...] = first[...]
    higher[...] = rest[...]


def departing_pages(latent_pool, page_moves):
    block = (1,) + latent_pool.shape[1:]
    moving = page_moves.shape[1] // 2
    shape = jax.ShapeDtypeStruct((moving,) + latent_pool.shape[1:], latent_pool.dtype)
    return pl.pallas_call(
        page_kernel,
        out_shape=(shape, shape),
        grid_spec=pltpu.PrefetchScalarGridSpec(
            num_scalar_prefetch=1,
            grid=(moving,),
            in_specs=[
                pl.BlockSpec(block, lambda i, moves: (moves[0, i], 0, 0)),
                pl.BlockSpec(block, lambda i, moves: (moves[0, moving + i], 0, 0)),
            ],
            out_specs=[pl.BlockSpec(block, lambda i, moves: (i, 0, 0))] * 2,
        ),
        cost_estimate=pl.CostEstimate(
            flops=0, bytes_accessed=8 * moving * block[1] * block[2], transcendentals=0
        ),
    )(page_moves, latent_pool, latent_pool)


def attention_kernel(page_list, lengths, queries, pool, low, high, out, rows):
    count, page = page_list.shape[1], pool.shape[1]
    moving = low.shape[0]
    for j in range(count):
        number = page_list[0, j]
        if j < 2 * moving:
            number = number - pool.shape[0]
            upper = number >= moving
            from_low = low[jnp.where(upper, 0, number)]
            from_high = high[jnp.where(upper, number - moving, 0)]
            block = jnp.where(upper, from_high, from_low)
        else:
            block = pool[number]
        rows[j * page : (j + 1) * page, :] = block
    scores = lax.dot_general(
        queries[0], rows[...], (((1,), (1,)), ((), ())), preferred_element_type=jnp.float32
    )
    place = lax.broadcasted_iota(jnp.int32, scores.shape, 1)
    scores = jnp.where(place < lengths[0], scores * softmax_scale, -1e30)
    values = jnp.exp(scores - jnp.max(scores, axis=1, keepdims=True))
    weights = (values / jnp.sum(values, axis=1, keepdims=True)).astype(jnp.bfloat16)
    mixed = jnp.dot(weights, rows[:, : out.shape[2]], preferred_element_type=jnp.float32)
    out[0] = mixed.astype(out.dtype)


def attention(queries, latent_pool, low, high, page_list, lengths):
    _, heads, width = queries.shape
    count = page_list.shape[1] * latent_pool.shape[1]
    return pl.pallas_call(
        attention_kernel,
        out_shape=jax.ShapeDtypeStruct((1, heads, KVL), jnp.bfloat16),
        in_specs=[pl.BlockSpec(memory_space=pltpu.SMEM)] * 2 + whole(4),
        out_specs=pl.BlockSpec(memory_space=pltpu.VMEM),
        scratch_shapes=[pltpu.VMEM((count, width), jnp.bfloat16)],
        compiler_params=pltpu.CompilerParams(vmem_limit_bytes=16 << 20),
        cost_estimate=pl.CostEstimate(
            flops=2 * heads * count * (width + KVL),
            bytes_accessed=2 * (latent_pool.size + 2 * queries.size),
            transcendentals=heads * count,
        ),
    )(page_list, lengths, queries, latent_pool, low, high)


def prepare_kernel(tokens, chosen, affinity, out):
    members, _, lanes = out.shape
    row = tokens[...].astype(jnp.float32)
    choices = chosen.shape[2]
    routing = [chosen[0].astype(jnp.float32), affinity[0].astype(jnp.float32)]
    routing.append(jnp.zeros((1, 2 * lanes - SLICE - 2 * choices), jnp.float32))
    for p in range(members):
        first = row[:, p * SLICE : p * SLICE + lanes]
        second = [row[:, p * SLICE + lanes : (p + 1) * SLICE]] + routing
        pair = [first, jnp.concatenate(second, axis=1)]
        out[p] = jnp.concatenate(pair, axis=0).astype(out.dtype)


def prepared(tokens, expert_ids, affinity, members):
    return pl.pallas_call(
        prepare_kernel,
        out_shape=jax.ShapeDtypeStruct((members, 2, WIDE // 2), jnp.bfloat16),
        in_specs=whole(3),
        out_specs=pl.BlockSpec(memory_space=pltpu.VMEM),
        cost_estimate=pl.CostEstimate(
            flops=0, bytes_accessed=4 * tokens.size, transcendentals=0
        ),
    )(tokens, expert_ids, affinity)


def sum_kernel(kept, given, out):
    out[...] = (kept[...] + given[...].astype(jnp.float32)).astype(out.dtype).reshape(out.shape)


def added(kept, given, groups):
    rows, width = kept.shape
    return pl.pallas_call(
        sum_kernel,
        out_shape=jax.ShapeDtypeStruct((groups, rows // groups, width), jnp.bfloat16),
        in_specs=whole(2),
        out_specs=pl.BlockSpec(memory_space=pltpu.VMEM),
        cost_estimate=pl.CostEstimate(
            flops=kept.size, bytes_accessed=8 * kept.size, transcendentals=0
        ),
    )(kept, given)


def shards(
    tokens,
    expert_ids,
    affinity,
    gate_up_blocks,
    down_blocks,
    queries,
    latent_pool,
    page_moves,
    page_list,
    lengths,
):
    members = lax.axis_size(EP)
    groups = lax.axis_size("z")
    chips = lax.axis_size(HALF) // 2
    choices = expert_ids.shape[2]
    capacity = members * choices // groups
    rows = groups * capacity
    units = gate_up_blocks.shape[3] // 2
    core = lax.axis_index("c")
    held = exchanged(prepared(tokens, expert_ids, affinity, members), EP)
    held, page_moves = lax.optimization_barrier((held, page_moves))
    held = held.reshape(members, WIDE)
    chosen = held[:, SLICE : SLICE + choices].astype(jnp.float32)
    affinity_all = held[:, SLICE + choices : SLICE + 2 * choices].astype(jnp.float32)
    route_weights = routed_scale * affinity_all / jnp.sum(affinity_all, axis=1, keepdims=True)
    matches = chosen[:, :, None] == jnp.arange(groups, dtype=jnp.float32)[None, None, :]
    member = jnp.any(matches, axis=1)
    weight_of = jnp.sum(jnp.where(matches, route_weights[:, :, None], 0.0), axis=1)
    earlier = jnp.arange(members)[:, None] > jnp.arange(members)[None, :]
    position = jnp.dot(
        earlier.astype(jnp.bfloat16),
        member.astype(jnp.bfloat16),
        preferred_element_type=jnp.float32,
    )
    slot_number = jnp.arange(capacity, dtype=jnp.float32)
    selector = member.T[:, None, :] & (position.T[:, None, :] == slot_number[None, :, None])
    sent_rows = jnp.dot(
        selector.astype(jnp.bfloat16).reshape(rows, members),
        held[:, :SLICE],
        preferred_element_type=jnp.float32,
    ).astype(jnp.bfloat16)
    arrived = exchanged(sent_rows.reshape(groups, capacity, SLICE), "z").reshape(rows, SLICE)
    to_lower, to_higher = departing_pages(latent_pool, page_moves)
    forward = [(i, (i + 1) % members) for i in range(members)]
    backward = [(target, source) for source, target in forward]
    low = lax.ppermute(to_higher, EP, forward)
    high = lax.ppermute(to_lower, EP, backward)
    arrived, low, high = lax.optimization_barrier((arrived, low, high))
    same_core = exchanged(jnp.broadcast_to(arrived[None], (chips, rows, SLICE)), ("y", "x"))
    down = down_blocks.reshape(units, chips, 2, SLICE).transpose(1, 2, 0, 3)
    down, same_core = lax.optimization_barrier((down, same_core))
    down = exchanged(down, ("y", "x"))
    other_core = lax.ppermute(same_core, "c", [(0, 1), (1, 0)])
    by_core = gate_up_blocks.reshape(chips, 2, SLICE, 2 * units)
    same_weights = lax.dynamic_index_in_dim(by_core, core, 1, keepdims=False)
    other_weights = lax.dynamic_index_in_dim(by_core, 1 - core, 1, keepdims=False)
    partial_sum = jnp.einsum(
        "urk,ukn->rn", same_core, same_weights, preferred_element_type=jnp.float32
    ) + jnp.einsum("urk,ukn->rn", other_core, other_weights, preferred_element_type=jnp.float32)
    partner_sum = lax.ppermute(partial_sum.astype(jnp.bfloat16), "h", [(0, 1), (1, 0)])
    activation = activated(partial_sum, partner_sum, chips)
    activation, down = lax.optimization_barrier((activation, down))
    activation = exchanged(activation, ("y", "x"))
    kept, given = down_sums(core.reshape(1).astype(jnp.int32), activation, down)
    summed = added(kept, lax.ppermute(given, "c", [(0, 1), (1, 0)]), groups)
    summed, low, high = lax.optimization_barrier((summed, low, high))
    attention_latent = attention(queries, latent_pool, low, high, page_list, lengths)
    returned = exchanged(summed, "z").reshape(rows, SLICE)
    returned, attention_latent = lax.optimization_barrier((returned, attention_latent))
    weighted = jnp.where(selector, weight_of.T[:, None, :], 0.0).reshape(rows, members)
    mixed = jnp.einsum(
        "rn,rk->nk", weighted, returned.astype(jnp.float32), precision=lax.Precision.HIGHEST
    )
    expert_mix = exchanged(mixed.astype(jnp.bfloat16), EP).reshape(1, -1)
    return (attention_latent, expert_mix)


def solution(mesh):
    fine = Mesh(mesh.devices.reshape(32, 2, 2, 4, 2), ("z",) + EP)
    both = ("z",) + EP
    placed = (
        P(both, None),
        P("z", EP, None),
        P("z", EP, None),
        P("z", EP, None, None),
        P("z", EP, None, None),
        P(both, None, None),
        P(both, None, None),
        P(both, None),
        P(both, None),
        P(both),
    )
    return jax.shard_map(
        shards,
        mesh=fine,
        in_specs=placed,
        out_specs=(P(both, None, None), P(both, None)),
        check_vma=False,
    )
```

```python
import jax
import jax.numpy as jnp
from jax import lax
from jax.experimental import pallas as pl
from jax.experimental.pallas import tpu as pltpu
from jax.sharding import Mesh, PartitionSpec as P

KVL = 512
SLICE = 224
WIDE = 256
HALF = ("y", "x", "c")
EP = ("h",) + HALF
MINOR = (((1,), (1,)), ((), ()))


softmax_scale = 192.0 ** (-0.5)
routed_scale = 2.5


def exchanged(value, axes):
    return lax.all_to_all(value, axes, split_axis=0, concat_axis=0, tiled=True)


def given_kernel(core, own, partner, weights, values, given):
    theirs = 1 - core[0]
    units = values.shape[1]
    sums = own[...] + partner[...].astype(jnp.float32)
    value = jax.nn.silu(sums[:, :units]) * sums[:, units:]
    values[...] = value.astype(values.dtype)
    for i in range(weights.shape[0]):
        given[i] = lax.dot_general(
            weights[i, theirs], values[...], MINOR, preferred_element_type=jnp.float32
        ).astype(given.dtype)


def given_sums(core, own, partner, weights):
    rows, columns = own.shape
    chips, _, width, units = weights.shape
    return pl.pallas_call(
        given_kernel,
        out_shape=(
            jax.ShapeDtypeStruct((rows, units), jnp.bfloat16),
            jax.ShapeDtypeStruct((chips, width, rows), jnp.bfloat16),
        ),
        in_specs=[pl.BlockSpec(memory_space=pltpu.SMEM)] + whole(3),
        out_specs=tuple(whole(2)),
        compiler_params=pltpu.CompilerParams(vmem_limit_bytes=24 << 20),
        cost_estimate=pl.CostEstimate(
            flops=2 * chips * rows * width * units,
            bytes_accessed=2 * weights.size + 6 * own.size + 2 * chips * rows * width,
            transcendentals=rows * units,
        ),
    )(core, own, partner, weights)


def kept_kernel(core, values, weights, received, out):
    mine = core[0]
    for i in range(weights.shape[0]):
        sums = lax.dot_general(
            weights[i, mine], values[...], MINOR, preferred_element_type=jnp.float32
        )
        out[i] = (sums + received[i].astype(jnp.float32)).astype(out.dtype)


def kept_sums(core, values, weights, received):
    chips, _, width, units = weights.shape
    rows = values.shape[0]
    return pl.pallas_call(
        kept_kernel,
        out_shape=jax.ShapeDtypeStruct((chips, width, rows), jnp.bfloat16),
        in_specs=[pl.BlockSpec(memory_space=pltpu.SMEM)] + whole(3),
        out_specs=pl.BlockSpec(memory_space=pltpu.VMEM),
        compiler_params=pltpu.CompilerParams(vmem_limit_bytes=24 << 20),
        cost_estimate=pl.CostEstimate(
            flops=2 * chips * rows * width * units,
            bytes_accessed=2 * weights.size + 4 * chips * rows * width,
            transcendentals=0,
        ),
    )(core, values, weights, received)


def whole(count):
    return [pl.BlockSpec(memory_space=pltpu.VMEM)] * count


def page_kernel(moves, first, rest, lower, higher):
    lower[...] = first[...]
    higher[...] = rest[...]


def departing_pages(latent_pool, page_moves):
    block = (1,) + latent_pool.shape[1:]
    moving = page_moves.shape[1] // 2
    shape = jax.ShapeDtypeStruct((moving,) + latent_pool.shape[1:], latent_pool.dtype)
    return pl.pallas_call(
        page_kernel,
        out_shape=(shape, shape),
        grid_spec=pltpu.PrefetchScalarGridSpec(
            num_scalar_prefetch=1,
            grid=(moving,),
            in_specs=[
                pl.BlockSpec(block, lambda i, moves: (moves[0, i], 0, 0)),
                pl.BlockSpec(block, lambda i, moves: (moves[0, moving + i], 0, 0)),
            ],
            out_specs=[pl.BlockSpec(block, lambda i, moves: (i, 0, 0))] * 2,
        ),
        cost_estimate=pl.CostEstimate(
            flops=0, bytes_accessed=8 * moving * block[1] * block[2], transcendentals=0
        ),
    )(page_moves, latent_pool, latent_pool)


def attention_kernel(page_list, lengths, queries, pool, low, high, out, rows):
    count, page = page_list.shape[1], pool.shape[1]
    moving = low.shape[0]
    for j in range(count):
        number = page_list[0, j]
        if j < 2 * moving:
            number = number - pool.shape[0]
            upper = number >= moving
            from_low = low[jnp.where(upper, 0, number)]
            from_high = high[jnp.where(upper, number - moving, 0)]
            block = jnp.where(upper, from_high, from_low)
        else:
            block = pool[number]
        rows[j * page : (j + 1) * page, :] = block
    scores = lax.dot_general(
        queries[0], rows[...], (((1,), (1,)), ((), ())), preferred_element_type=jnp.float32
    )
    place = lax.broadcasted_iota(jnp.int32, scores.shape, 1)
    scores = jnp.where(place < lengths[0], scores * softmax_scale, -1e30)
    values = jnp.exp(scores - jnp.max(scores, axis=1, keepdims=True))
    weights = (values / jnp.sum(values, axis=1, keepdims=True)).astype(jnp.bfloat16)
    mixed = jnp.dot(weights, rows[:, : out.shape[2]], preferred_element_type=jnp.float32)
    out[0] = mixed.astype(out.dtype)


def attention(queries, latent_pool, low, high, page_list, lengths):
    _, heads, width = queries.shape
    count = page_list.shape[1] * latent_pool.shape[1]
    return pl.pallas_call(
        attention_kernel,
        out_shape=jax.ShapeDtypeStruct((1, heads, KVL), jnp.bfloat16),
        in_specs=[pl.BlockSpec(memory_space=pltpu.SMEM)] * 2 + whole(4),
        out_specs=pl.BlockSpec(memory_space=pltpu.VMEM),
        scratch_shapes=[pltpu.VMEM((count, width), jnp.bfloat16)],
        compiler_params=pltpu.CompilerParams(vmem_limit_bytes=16 << 20),
        cost_estimate=pl.CostEstimate(
            flops=2 * heads * count * (width + KVL),
            bytes_accessed=2 * (latent_pool.size + 2 * queries.size),
            transcendentals=heads * count,
        ),
    )(page_list, lengths, queries, latent_pool, low, high)


def prepare_kernel(tokens, chosen, affinity, out):
    members, _, lanes = out.shape
    row = tokens[...].astype(jnp.float32)
    choices = chosen.shape[2]
    routing = [chosen[0].astype(jnp.float32), affinity[0].astype(jnp.float32)]
    routing.append(jnp.zeros((1, 2 * lanes - SLICE - 2 * choices), jnp.float32))
    for p in range(members):
        first = row[:, p * SLICE : p * SLICE + lanes]
        second = [row[:, p * SLICE + lanes : (p + 1) * SLICE]] + routing
        pair = [first, jnp.concatenate(second, axis=1)]
        out[p] = jnp.concatenate(pair, axis=0).astype(out.dtype)


def prepared(tokens, expert_ids, affinity, members):
    return pl.pallas_call(
        prepare_kernel,
        out_shape=jax.ShapeDtypeStruct((members, 2, WIDE // 2), jnp.bfloat16),
        in_specs=whole(3),
        out_specs=pl.BlockSpec(memory_space=pltpu.VMEM),
        cost_estimate=pl.CostEstimate(
            flops=0, bytes_accessed=4 * tokens.size, transcendentals=0
        ),
    )(tokens, expert_ids, affinity)


def sum_kernel(parts, out):
    sums = parts[0].astype(jnp.float32)
    for n in range(1, parts.shape[0]):
        sums += parts[n].astype(jnp.float32)
    out[...] = sums.T.reshape(out.shape).astype(out.dtype)


def added(parts, groups):
    _, width, rows = parts.shape
    return pl.pallas_call(
        sum_kernel,
        out_shape=jax.ShapeDtypeStruct((groups, rows // groups, width), jnp.bfloat16),
        in_specs=whole(1),
        out_specs=pl.BlockSpec(memory_space=pltpu.VMEM),
        compiler_params=pltpu.CompilerParams(vmem_limit_bytes=24 << 20),
        cost_estimate=pl.CostEstimate(
            flops=parts.size, bytes_accessed=2 * parts.size, transcendentals=0
        ),
    )(parts)


def shards(
    tokens,
    expert_ids,
    affinity,
    gate_up_blocks,
    down_blocks,
    queries,
    latent_pool,
    page_moves,
    page_list,
    lengths,
):
    members = lax.axis_size(EP)
    groups = lax.axis_size("z")
    chips = lax.axis_size(HALF) // 2
    choices = expert_ids.shape[2]
    capacity = members * choices // groups
    rows = groups * capacity
    units = gate_up_blocks.shape[3] // 2
    core = lax.axis_index("c")
    held = exchanged(prepared(tokens, expert_ids, affinity, members), EP)
    held, page_moves = lax.optimization_barrier((held, page_moves))
    held = held.reshape(members, WIDE)
    chosen = held[:, SLICE : SLICE + choices].astype(jnp.float32)
    affinity_all = held[:, SLICE + choices : SLICE + 2 * choices].astype(jnp.float32)
    route_weights = routed_scale * affinity_all / jnp.sum(affinity_all, axis=1, keepdims=True)
    matches = chosen[:, :, None] == jnp.arange(groups, dtype=jnp.float32)[None, None, :]
    member = jnp.any(matches, axis=1)
    weight_of = jnp.sum(jnp.where(matches, route_weights[:, :, None], 0.0), axis=1)
    earlier = jnp.arange(members)[:, None] > jnp.arange(members)[None, :]
    position = jnp.dot(
        earlier.astype(jnp.bfloat16),
        member.astype(jnp.bfloat16),
        preferred_element_type=jnp.float32,
    )
    slot_number = jnp.arange(capacity, dtype=jnp.float32)
    selector = member.T[:, None, :] & (position.T[:, None, :] == slot_number[None, :, None])
    sent_rows = jnp.dot(
        selector.astype(jnp.bfloat16).reshape(rows, members),
        held[:, :SLICE],
        preferred_element_type=jnp.float32,
    ).astype(jnp.bfloat16)
    arrived = exchanged(sent_rows.reshape(groups, capacity, SLICE), "z").reshape(rows, SLICE)
    to_lower, to_higher = departing_pages(latent_pool, page_moves)
    forward = [(i, (i + 1) % members) for i in range(members)]
    backward = [(target, source) for source, target in forward]
    low = lax.ppermute(to_higher, EP, forward)
    high = lax.ppermute(to_lower, EP, backward)
    arrived, low, high = lax.optimization_barrier((arrived, low, high))
    same_core = exchanged(jnp.broadcast_to(arrived[None], (chips, rows, SLICE)), ("y", "x"))
    other_core = lax.ppermute(same_core, "c", [(0, 1), (1, 0)])
    by_core = gate_up_blocks.reshape(chips, 2, SLICE, 2 * units)
    same_weights = lax.dynamic_index_in_dim(by_core, core, 1, keepdims=False)
    other_weights = lax.dynamic_index_in_dim(by_core, 1 - core, 1, keepdims=False)
    partial_sum = jnp.einsum(
        "urk,ukn->rn", same_core, same_weights, preferred_element_type=jnp.float32
    ) + jnp.einsum("urk,ukn->rn", other_core, other_weights, preferred_element_type=jnp.float32)
    partner_sum = lax.ppermute(partial_sum.astype(jnp.bfloat16), "h", [(0, 1), (1, 0)])
    down = down_blocks.reshape(units, chips, 2, SLICE).transpose(1, 2, 3, 0)
    core = core.reshape(1).astype(jnp.int32)
    values, given = given_sums(core, partial_sum, partner_sum, down)
    received = lax.ppermute(given, "c", [(0, 1), (1, 0)])
    summed = added(exchanged(kept_sums(core, values, down, received), ("y", "x")), groups)
    summed, low, high = lax.optimization_barrier((summed, low, high))
    attention_latent = attention(queries, latent_pool, low, high, page_list, lengths)
    returned = exchanged(summed, "z").reshape(rows, SLICE)
    returned, attention_latent = lax.optimization_barrier((returned, attention_latent))
    weighted = jnp.where(selector, weight_of.T[:, None, :], 0.0).reshape(rows, members)
    mixed = jnp.einsum(
        "rn,rk->nk", weighted, returned.astype(jnp.float32), precision=lax.Precision.HIGHEST
    )
    expert_mix = exchanged(mixed.astype(jnp.bfloat16), EP).reshape(1, -1)
    return (attention_latent, expert_mix)


def solution(mesh):
    fine = Mesh(mesh.devices.reshape(32, 2, 2, 4, 2), ("z",) + EP)
    both = ("z",) + EP
    placed = (
        P(both, None),
        P("z", EP, None),
        P("z", EP, None),
        P("z", EP, None, None),
        P("z", EP, None, None),
        P(both, None, None),
        P(both, None, None),
        P(both, None),
        P(both, None),
        P(both),
    )
    return jax.shard_map(
        shards,
        mesh=fine,
        in_specs=placed,
        out_specs=(P(both, None, None), P(both, None)),
        check_vma=False,
    )
```

```python
import jax
import jax.numpy as jnp
from jax import lax
from jax.experimental import pallas as pl
from jax.experimental.pallas import tpu as pltpu
from jax.sharding import Mesh, PartitionSpec as P

KVL = 512
EP = ("h", "y", "x", "c")
MINOR = (((1,), (1,)), ((), ()))
MAJOR = (((0,), (0,)), ((), ()))


softmax_scale = 192.0 ** (-0.5)
routed_scale = 2.5


def exchanged(value, axes):
    return lax.all_to_all(value, axes, split_axis=0, concat_axis=0, tiled=True)


def gate_up_kernel(values, own, other, sums, rounded):
    chips = values.shape[0]
    for n, weights in enumerate((own, other)):
        columns = weights.shape[2]
        total = jnp.zeros((values.shape[2], columns), jnp.float32)
        for i in range(chips):
            total += lax.dot_general(
                values[i], weights[i], MAJOR, preferred_element_type=jnp.float32
            )
        sums[:, n * columns : (n + 1) * columns] = total
        rounded[:, n * columns : (n + 1) * columns] = total.astype(rounded.dtype)


def gate_up_sums(values, own, other):
    chips, width, rows = values.shape
    columns = 2 * own.shape[2]
    return pl.pallas_call(
        gate_up_kernel,
        out_shape=(
            jax.ShapeDtypeStruct((rows, columns), jnp.float32),
            jax.ShapeDtypeStruct((rows, columns), jnp.bfloat16),
        ),
        in_specs=whole(3),
        out_specs=tuple(whole(2)),
        compiler_params=pltpu.CompilerParams(vmem_limit_bytes=24 << 20),
        cost_estimate=pl.CostEstimate(
            flops=2 * chips * rows * width * columns,
            bytes_accessed=4 * own.size + 2 * values.size + 6 * rows * columns,
            transcendentals=0,
        ),
    )(values, own, other)


def down_kernel(sums, partner, own, other, out):
    units = own.shape[2]
    total = sums[...] + partner[...].astype(jnp.float32)
    values = []
    for n in range(2):
        gate = total[:, 2 * n * units : (2 * n + 1) * units]
        up = total[:, (2 * n + 1) * units : (2 * n + 2) * units]
        values.append((jax.nn.silu(gate) * up).astype(jnp.bfloat16))
    for i in range(out.shape[0]):
        mixed = lax.dot_general(own[i], values[0], MINOR, preferred_element_type=jnp.float32)
        mixed += lax.dot_general(other[i], values[1], MINOR, preferred_element_type=jnp.float32)
        out[i] = mixed.astype(out.dtype)


def down_sums(sums, partner, own, other):
    chips, width, units = own.shape
    rows = sums.shape[0]
    return pl.pallas_call(
        down_kernel,
        out_shape=jax.ShapeDtypeStruct((chips, width, rows), jnp.bfloat16),
        in_specs=whole(4),
        out_specs=pl.BlockSpec(memory_space=pltpu.VMEM),
        compiler_params=pltpu.CompilerParams(vmem_limit_bytes=24 << 20),
        cost_estimate=pl.CostEstimate(
            flops=4 * chips * rows * width * units,
            bytes_accessed=4 * own.size + 6 * sums.size + 2 * chips * rows * width,
            transcendentals=2 * rows * units,
        ),
    )(sums, partner, own, other)


def whole(count):
    return [pl.BlockSpec(memory_space=pltpu.VMEM)] * count


def page_kernel(moves, first, rest, lower, higher):
    lower[...] = first[...]
    higher[...] = rest[...]


def departing_pages(latent_pool, page_moves):
    block = (1,) + latent_pool.shape[1:]
    moving = page_moves.shape[1] // 2
    shape = jax.ShapeDtypeStruct((moving,) + latent_pool.shape[1:], latent_pool.dtype)
    return pl.pallas_call(
        page_kernel,
        out_shape=(shape, shape),
        grid_spec=pltpu.PrefetchScalarGridSpec(
            num_scalar_prefetch=1,
            grid=(moving,),
            in_specs=[
                pl.BlockSpec(block, lambda i, moves: (moves[0, i], 0, 0)),
                pl.BlockSpec(block, lambda i, moves: (moves[0, moving + i], 0, 0)),
            ],
            out_specs=[pl.BlockSpec(block, lambda i, moves: (i, 0, 0))] * 2,
        ),
        cost_estimate=pl.CostEstimate(
            flops=0, bytes_accessed=8 * moving * block[1] * block[2], transcendentals=0
        ),
    )(page_moves, latent_pool, latent_pool)


def attention_kernel(page_list, lengths, queries, pool, low, high, out, rows):
    count, page = page_list.shape[1], pool.shape[1]
    moving = low.shape[0]
    for j in range(count):
        number = page_list[0, j]
        if j < 2 * moving:
            number = number - pool.shape[0]
            upper = number >= moving
            from_low = low[jnp.where(upper, 0, number)]
            from_high = high[jnp.where(upper, number - moving, 0)]
            block = jnp.where(upper, from_high, from_low)
        else:
            block = pool[number]
        rows[j * page : (j + 1) * page, :] = block
    scores = lax.dot_general(
        queries[0], rows[...], (((1,), (1,)), ((), ())), preferred_element_type=jnp.float32
    )
    place = lax.broadcasted_iota(jnp.int32, scores.shape, 1)
    scores = jnp.where(place < lengths[0], scores * softmax_scale, -1e30)
    values = jnp.exp(scores - jnp.max(scores, axis=1, keepdims=True))
    weights = (values / jnp.sum(values, axis=1, keepdims=True)).astype(jnp.bfloat16)
    mixed = jnp.dot(weights, rows[:, : out.shape[2]], preferred_element_type=jnp.float32)
    out[0] = mixed.astype(out.dtype)


def attention(queries, latent_pool, low, high, page_list, lengths):
    _, heads, width = queries.shape
    count = page_list.shape[1] * latent_pool.shape[1]
    return pl.pallas_call(
        attention_kernel,
        out_shape=jax.ShapeDtypeStruct((1, heads, KVL), jnp.bfloat16),
        in_specs=[pl.BlockSpec(memory_space=pltpu.SMEM)] * 2 + whole(4),
        out_specs=pl.BlockSpec(memory_space=pltpu.VMEM),
        scratch_shapes=[pltpu.VMEM((count, width), jnp.bfloat16)],
        compiler_params=pltpu.CompilerParams(vmem_limit_bytes=16 << 20),
        cost_estimate=pl.CostEstimate(
            flops=2 * heads * count * (width + KVL),
            bytes_accessed=2 * (latent_pool.size + 2 * queries.size),
            transcendentals=heads * count,
        ),
    )(page_list, lengths, queries, latent_pool, low, high)


def prepare_kernel(tokens, chosen, affinity, out):
    chips, lines, lanes = out.shape[0] // 2, out.shape[1], out.shape[2]
    row = tokens[...].astype(jnp.float32)
    width = row.shape[1] // chips
    choices = chosen.shape[2]
    routing = [chosen[0].astype(jnp.float32), affinity[0].astype(jnp.float32)]
    routing.append(jnp.zeros((1, lines * lanes - width - 2 * choices), jnp.float32))
    for p in range(chips):
        start = p * width
        block = [row[:, start + n * lanes : start + (n + 1) * lanes] for n in range(lines - 1)]
        last = [row[:, start + (lines - 1) * lanes : start + width]] + routing
        block.append(jnp.concatenate(last, axis=1))
        block = jnp.concatenate(block, axis=0).astype(out.dtype)
        out[2 * p] = block
        out[2 * p + 1] = block


def prepared(tokens, expert_ids, affinity, members):
    return pl.pallas_call(
        prepare_kernel,
        out_shape=jax.ShapeDtypeStruct((members, 4, 128), jnp.bfloat16),
        in_specs=whole(3),
        out_specs=pl.BlockSpec(memory_space=pltpu.VMEM),
        cost_estimate=pl.CostEstimate(
            flops=0, bytes_accessed=4 * tokens.size, transcendentals=0
        ),
    )(tokens, expert_ids, affinity)


def sum_kernel(parts, out):
    sums = parts[0].astype(jnp.float32)
    for n in range(1, parts.shape[0]):
        sums += parts[n].astype(jnp.float32)
    out[...] = sums.T.reshape(out.shape).astype(out.dtype)


def added(parts, groups):
    _, width, rows = parts.shape
    return pl.pallas_call(
        sum_kernel,
        out_shape=jax.ShapeDtypeStruct((groups, rows // groups, width), jnp.bfloat16),
        in_specs=whole(1),
        out_specs=pl.BlockSpec(memory_space=pltpu.VMEM),
        compiler_params=pltpu.CompilerParams(vmem_limit_bytes=24 << 20),
        cost_estimate=pl.CostEstimate(
            flops=parts.size, bytes_accessed=2 * parts.size, transcendentals=0
        ),
    )(parts)


def shards(
    tokens,
    expert_ids,
    affinity,
    gate_up_blocks,
    down_blocks,
    queries,
    latent_pool,
    page_moves,
    page_list,
    lengths,
):
    members = lax.axis_size(EP)
    groups = lax.axis_size("z")
    chips = members // 4
    choices = expert_ids.shape[2]
    slots = members * choices // groups // 2
    rows = groups * slots
    units = gate_up_blocks.shape[3] // 2
    width = 2 * tokens.shape[1] // members
    between_cores = [(0, 1), (1, 0)]
    held = exchanged(prepared(tokens, expert_ids, affinity, members), EP)
    gate_up = gate_up_blocks.reshape(chips, width, 2 * units)
    other_gate_up = lax.ppermute(gate_up, "c", between_cores)
    held, page_moves, other_gate_up, down_blocks = lax.optimization_barrier(
        (held, page_moves, other_gate_up, down_blocks)
    )
    held = held.reshape(members, -1)
    chosen = held[:, width : width + choices].astype(jnp.float32)
    affinity_all = held[:, width + choices : width + 2 * choices].astype(jnp.float32)
    route_weights = routed_scale * affinity_all / jnp.sum(affinity_all, axis=1, keepdims=True)
    matches = chosen[:, :, None] == jnp.arange(groups, dtype=jnp.float32)[None, None, :]
    member = jnp.any(matches, axis=1)
    weight_of = jnp.sum(jnp.where(matches, route_weights[:, :, None], 0.0), axis=1)
    earlier = jnp.arange(members)[:, None] > jnp.arange(members)[None, :]
    position = jnp.dot(
        earlier.astype(jnp.bfloat16),
        member.astype(jnp.bfloat16),
        preferred_element_type=jnp.float32,
    )
    slot_number = (jnp.arange(slots) + lax.axis_index("c") * slots).astype(jnp.float32)
    selector = member.T[:, None, :] & (position.T[:, None, :] == slot_number[None, :, None])
    sent_rows = jnp.dot(
        selector.astype(jnp.bfloat16).reshape(rows, members),
        held[:, :width],
        preferred_element_type=jnp.float32,
    ).astype(jnp.bfloat16)
    arrived = exchanged(sent_rows.reshape(groups, slots, width), "z").reshape(rows, width)
    to_lower, to_higher = departing_pages(latent_pool, page_moves)
    forward = [(i, (i + 1) % members) for i in range(members)]
    backward = [(target, source) for source, target in forward]
    low = lax.ppermute(to_higher, EP, forward)
    high = lax.ppermute(to_lower, EP, backward)
    down = down_blocks.reshape(units, chips, width).transpose(1, 2, 0)
    arrived, low, high, down = lax.optimization_barrier((arrived, low, high, down))
    gathered = exchanged(jnp.broadcast_to(arrived.T[None], (chips, width, rows)), ("y", "x"))
    sums, rounded = gate_up_sums(gathered, gate_up, other_gate_up)
    rounded, down = lax.optimization_barrier((rounded, down))
    partner = lax.ppermute(rounded, "h", [(0, 1), (1, 0)])
    other_down = lax.ppermute(down, "c", between_cores)
    block_sums = down_sums(sums, partner, down, other_down)
    summed = added(exchanged(block_sums, ("y", "x")), groups)
    summed, low, high = lax.optimization_barrier((summed, low, high))
    attention_latent = attention(queries, latent_pool, low, high, page_list, lengths)
    returned = exchanged(summed, "z").reshape(rows, width)
    returned, attention_latent = lax.optimization_barrier((returned, attention_latent))
    weighted = jnp.where(selector, weight_of.T[:, None, :], 0.0).reshape(rows, members)
    mixed = jnp.einsum(
        "rn,rk->nk", weighted, returned.astype(jnp.float32), precision=lax.Precision.HIGHEST
    )
    halves = exchanged(mixed.astype(jnp.bfloat16), EP).reshape(members // 2, 2, width)
    expert_mix = jnp.sum(halves.astype(jnp.float32), axis=1).astype(jnp.bfloat16).reshape(1, -1)
    return (attention_latent, expert_mix)


def solution(mesh):
    fine = Mesh(mesh.devices.reshape(32, 2, 2, 4, 2), ("z",) + EP)
    both = ("z",) + EP
    placed = (
        P(both, None),
        P("z", EP, None),
        P("z", EP, None),
        P("z", EP, None, None),
        P("z", EP, None, None),
        P(both, None, None),
        P(both, None, None),
        P(both, None),
        P(both, None),
        P(both),
    )
    return jax.shard_map(
        shards,
        mesh=fine,
        in_specs=placed,
        out_specs=(P(both, None, None), P(both, None)),
        check_vma=False,
    )
```

```python
import jax
import jax.numpy as jnp
from jax import lax
from jax.experimental import pallas as pl
from jax.experimental.pallas import tpu as pltpu
from jax.sharding import Mesh, PartitionSpec as P

KVL = 512
EP = ("h", "y", "x", "c")
MINOR = (((1,), (1,)), ((), ()))
MAJOR = (((0,), (0,)), ((), ()))


softmax_scale = 192.0 ** (-0.5)
routed_scale = 2.5


def exchanged(value, axes):
    return lax.all_to_all(value, axes, split_axis=0, concat_axis=0, tiled=True)


def gate_up_kernel(values, own, other, sums, rounded):
    chips = values.shape[0]
    for n, weights in enumerate((own, other)):
        columns = weights.shape[2]
        total = jnp.zeros((values.shape[2], columns), jnp.float32)
        for i in range(chips):
            total += lax.dot_general(
                values[i], weights[i], MAJOR, preferred_element_type=jnp.float32
            )
        sums[:, n * columns : (n + 1) * columns] = total
        rounded[:, n * columns : (n + 1) * columns] = total.astype(rounded.dtype)


def gate_up_sums(values, own, other):
    chips, width, rows = values.shape
    columns = 2 * own.shape[2]
    return pl.pallas_call(
        gate_up_kernel,
        out_shape=(
            jax.ShapeDtypeStruct((rows, columns), jnp.float32),
            jax.ShapeDtypeStruct((rows, columns), jnp.bfloat16),
        ),
        in_specs=whole(3),
        out_specs=tuple(whole(2)),
        compiler_params=pltpu.CompilerParams(vmem_limit_bytes=24 << 20),
        cost_estimate=pl.CostEstimate(
            flops=2 * chips * rows * width * columns,
            bytes_accessed=4 * own.size + 2 * values.size + 6 * rows * columns,
            transcendentals=0,
        ),
    )(values, own, other)


def down_kernel(sums, partner, own, other, out):
    units = own.shape[2]
    total = sums[...] + partner[...].astype(jnp.float32)
    values = []
    for n in range(2):
        gate = total[:, 2 * n * units : (2 * n + 1) * units]
        up = total[:, (2 * n + 1) * units : (2 * n + 2) * units]
        values.append((jax.nn.silu(gate) * up).astype(jnp.bfloat16))
    for i in range(out.shape[0]):
        mixed = lax.dot_general(own[i], values[0], MINOR, preferred_element_type=jnp.float32)
        mixed += lax.dot_general(other[i], values[1], MINOR, preferred_element_type=jnp.float32)
        out[i] = mixed.astype(out.dtype)


def down_sums(sums, partner, own, other):
    chips, width, units = own.shape
    rows = sums.shape[0]
    return pl.pallas_call(
        down_kernel,
        out_shape=jax.ShapeDtypeStruct((chips, width, rows), jnp.bfloat16),
        in_specs=whole(4),
        out_specs=pl.BlockSpec(memory_space=pltpu.VMEM),
        compiler_params=pltpu.CompilerParams(vmem_limit_bytes=24 << 20),
        cost_estimate=pl.CostEstimate(
            flops=4 * chips * rows * width * units,
            bytes_accessed=4 * own.size + 6 * sums.size + 2 * chips * rows * width,
            transcendentals=2 * rows * units,
        ),
    )(sums, partner, own, other)


def whole(count):
    return [pl.BlockSpec(memory_space=pltpu.VMEM)] * count


def page_kernel(moves, first, rest, lower, higher):
    lower[...] = first[...]
    higher[...] = rest[...]


def departing_pages(latent_pool, page_moves):
    block = (1,) + latent_pool.shape[1:]
    moving = page_moves.shape[1] // 2
    shape = jax.ShapeDtypeStruct((moving,) + latent_pool.shape[1:], latent_pool.dtype)
    return pl.pallas_call(
        page_kernel,
        out_shape=(shape, shape),
        grid_spec=pltpu.PrefetchScalarGridSpec(
            num_scalar_prefetch=1,
            grid=(moving,),
            in_specs=[
                pl.BlockSpec(block, lambda i, moves: (moves[0, i], 0, 0)),
                pl.BlockSpec(block, lambda i, moves: (moves[0, moving + i], 0, 0)),
            ],
            out_specs=[pl.BlockSpec(block, lambda i, moves: (i, 0, 0))] * 2,
        ),
        cost_estimate=pl.CostEstimate(
            flops=0, bytes_accessed=8 * moving * block[1] * block[2], transcendentals=0
        ),
    )(page_moves, latent_pool, latent_pool)


def attention_kernel(page_list, lengths, queries, pool, low, high, out, rows):
    count, page = page_list.shape[1], pool.shape[1]
    moving = low.shape[0]
    for j in range(count):
        number = page_list[0, j]
        if j < 2 * moving:
            number = number - pool.shape[0]
            upper = number >= moving
            from_low = low[jnp.where(upper, 0, number)]
            from_high = high[jnp.where(upper, number - moving, 0)]
            block = jnp.where(upper, from_high, from_low)
        else:
            block = pool[number]
        rows[j * page : (j + 1) * page, :] = block
    scores = lax.dot_general(
        queries[0], rows[...], (((1,), (1,)), ((), ())), preferred_element_type=jnp.float32
    )
    place = lax.broadcasted_iota(jnp.int32, scores.shape, 1)
    scores = jnp.where(place < lengths[0], scores * softmax_scale, -1e30)
    values = jnp.exp(scores - jnp.max(scores, axis=1, keepdims=True))
    weights = (values / jnp.sum(values, axis=1, keepdims=True)).astype(jnp.bfloat16)
    mixed = jnp.dot(weights, rows[:, : out.shape[2]], preferred_element_type=jnp.float32)
    out[0] = mixed.astype(out.dtype)


def attention(queries, latent_pool, low, high, page_list, lengths):
    _, heads, width = queries.shape
    count = page_list.shape[1] * latent_pool.shape[1]
    return pl.pallas_call(
        attention_kernel,
        out_shape=jax.ShapeDtypeStruct((1, heads, KVL), jnp.bfloat16),
        in_specs=[pl.BlockSpec(memory_space=pltpu.SMEM)] * 2 + whole(4),
        out_specs=pl.BlockSpec(memory_space=pltpu.VMEM),
        scratch_shapes=[pltpu.VMEM((count, width), jnp.bfloat16)],
        compiler_params=pltpu.CompilerParams(vmem_limit_bytes=16 << 20),
        cost_estimate=pl.CostEstimate(
            flops=2 * heads * count * (width + KVL),
            bytes_accessed=2 * (latent_pool.size + 2 * queries.size),
            transcendentals=heads * count,
        ),
    )(page_list, lengths, queries, latent_pool, low, high)


def prepare_kernel(tokens, chosen, affinity, out):
    chips, lines, lanes = out.shape[0] // 2, out.shape[1], out.shape[2]
    row = tokens[...].astype(jnp.float32)
    width = row.shape[1] // chips
    choices = chosen.shape[2]
    routing = [chosen[0].astype(jnp.float32), affinity[0].astype(jnp.float32)]
    routing.append(jnp.zeros((1, lines * lanes - width - 2 * choices), jnp.float32))
    for p in range(chips):
        start = p * width
        block = [row[:, start + n * lanes : start + (n + 1) * lanes] for n in range(lines - 1)]
        last = [row[:, start + (lines - 1) * lanes : start + width]] + routing
        block.append(jnp.concatenate(last, axis=1))
        block = jnp.concatenate(block, axis=0).astype(out.dtype)
        out[2 * p] = block
        out[2 * p + 1] = block


def prepared(tokens, expert_ids, affinity, members):
    return pl.pallas_call(
        prepare_kernel,
        out_shape=jax.ShapeDtypeStruct((members, 4, 128), jnp.bfloat16),
        in_specs=whole(3),
        out_specs=pl.BlockSpec(memory_space=pltpu.VMEM),
        cost_estimate=pl.CostEstimate(
            flops=0, bytes_accessed=4 * tokens.size, transcendentals=0
        ),
    )(tokens, expert_ids, affinity)


def sum_kernel(parts, out):
    sums = parts[0].astype(jnp.float32)
    for n in range(1, parts.shape[0]):
        sums += parts[n].astype(jnp.float32)
    out[...] = sums.T.reshape(out.shape).astype(out.dtype)


def added(parts, groups):
    _, width, rows = parts.shape
    return pl.pallas_call(
        sum_kernel,
        out_shape=jax.ShapeDtypeStruct((groups, rows // groups, width), jnp.bfloat16),
        in_specs=whole(1),
        out_specs=pl.BlockSpec(memory_space=pltpu.VMEM),
        compiler_params=pltpu.CompilerParams(vmem_limit_bytes=24 << 20),
        cost_estimate=pl.CostEstimate(
            flops=parts.size, bytes_accessed=2 * parts.size, transcendentals=0
        ),
    )(parts)


def shards(
    tokens,
    expert_ids,
    affinity,
    gate_up_blocks,
    down_blocks,
    queries,
    latent_pool,
    page_moves,
    page_list,
    lengths,
):
    members = lax.axis_size(EP)
    groups = lax.axis_size("z")
    chips = members // 4
    choices = expert_ids.shape[2]
    slots = members * choices // groups // 2
    rows = groups * slots
    units = gate_up_blocks.shape[3] // 2
    width = 2 * tokens.shape[1] // members
    between_cores = [(0, 1), (1, 0)]
    held = exchanged(prepared(tokens, expert_ids, affinity, members), EP)
    gate_up = gate_up_blocks.reshape(chips, width, 2 * units)
    other_gate_up = lax.ppermute(gate_up, "c", between_cores)
    other_down = lax.ppermute(down_blocks, "c", between_cores)
    held, page_moves, other_gate_up, down_blocks, other_down = lax.optimization_barrier(
        (held, page_moves, other_gate_up, down_blocks, other_down)
    )
    held = held.reshape(members, -1)
    chosen = held[:, width : width + choices].astype(jnp.float32)
    affinity_all = held[:, width + choices : width + 2 * choices].astype(jnp.float32)
    route_weights = routed_scale * affinity_all / jnp.sum(affinity_all, axis=1, keepdims=True)
    matches = chosen[:, :, None] == jnp.arange(groups, dtype=jnp.float32)[None, None, :]
    member = jnp.any(matches, axis=1)
    weight_of = jnp.sum(jnp.where(matches, route_weights[:, :, None], 0.0), axis=1)
    earlier = jnp.arange(members)[:, None] > jnp.arange(members)[None, :]
    position = jnp.dot(
        earlier.astype(jnp.bfloat16),
        member.astype(jnp.bfloat16),
        preferred_element_type=jnp.float32,
    )
    slot_number = (jnp.arange(slots) + lax.axis_index("c") * slots).astype(jnp.float32)
    selector = member.T[:, None, :] & (position.T[:, None, :] == slot_number[None, :, None])
    sent_rows = jnp.dot(
        selector.astype(jnp.bfloat16).reshape(rows, members),
        held[:, :width],
        preferred_element_type=jnp.float32,
    ).astype(jnp.bfloat16)
    arrived = exchanged(sent_rows.reshape(groups, slots, width), "z").reshape(rows, width)
    to_lower, to_higher = departing_pages(latent_pool, page_moves)
    forward = [(i, (i + 1) % members) for i in range(members)]
    backward = [(target, source) for source, target in forward]
    low = lax.ppermute(to_higher, EP, forward)
    high = lax.ppermute(to_lower, EP, backward)
    down = down_blocks.reshape(units, chips, width).transpose(1, 2, 0)
    other_down = other_down.reshape(units, chips, width).transpose(1, 2, 0)
    arrived, low, high, down, other_down = lax.optimization_barrier(
        (arrived, low, high, down, other_down)
    )
    gathered = exchanged(jnp.broadcast_to(arrived.T[None], (chips, width, rows)), ("y", "x"))
    sums, rounded = gate_up_sums(gathered, gate_up, other_gate_up)
    partner = lax.ppermute(rounded, "h", [(0, 1), (1, 0)])
    block_sums = down_sums(sums, partner, down, other_down)
    summed = added(exchanged(block_sums, ("y", "x")), groups)
    summed, low, high = lax.optimization_barrier((summed, low, high))
    attention_latent = attention(queries, latent_pool, low, high, page_list, lengths)
    returned = exchanged(summed, "z").reshape(rows, width)
    returned, attention_latent = lax.optimization_barrier((returned, attention_latent))
    weighted = jnp.where(selector, weight_of.T[:, None, :], 0.0).reshape(rows, members)
    mixed = jnp.einsum(
        "rn,rk->nk", weighted, returned.astype(jnp.float32), precision=lax.Precision.HIGHEST
    )
    mixed = mixed.astype(jnp.bfloat16).reshape(members, 2, width // 2)
    halves = exchanged(mixed, EP).reshape(members // 2, 2, width)
    expert_mix = jnp.sum(halves.astype(jnp.float32), axis=1).astype(jnp.bfloat16).reshape(1, -1)
    return (attention_latent, expert_mix)


def solution(mesh):
    fine = Mesh(mesh.devices.reshape(32, 2, 2, 4, 2), ("z",) + EP)
    both = ("z",) + EP
    placed = (
        P(both, None),
        P("z", EP, None),
        P("z", EP, None),
        P("z", EP, None, None),
        P("z", EP, None, None),
        P(both, None, None),
        P(both, None, None),
        P(both, None),
        P(both, None),
        P(both),
    )
    return jax.shard_map(
        shards,
        mesh=fine,
        in_specs=placed,
        out_specs=(P(both, None, None), P(both, None)),
        check_vma=False,
    )
```

```python
import jax
import jax.numpy as jnp
from jax import lax
from jax.experimental import pallas as pl
from jax.experimental.pallas import tpu as pltpu
from jax.sharding import Mesh, PartitionSpec as P

KVL = 512
EP = ("h", "y", "x", "c")
MINOR = (((1,), (1,)), ((), ()))
MAJOR = (((0,), (0,)), ((), ()))


softmax_scale = 192.0 ** (-0.5)
routed_scale = 2.5


def exchanged(value, axes):
    return lax.all_to_all(value, axes, split_axis=0, concat_axis=0, tiled=True)


def gate_up_kernel(values, own, other, sums, rounded):
    chips = values.shape[0]
    for n, weights in enumerate((own, other)):
        columns = weights.shape[2]
        total = jnp.zeros((values.shape[2], columns), jnp.float32)
        for i in range(chips):
            total += lax.dot_general(
                values[i], weights[i], MAJOR, preferred_element_type=jnp.float32
            )
        sums[:, n * columns : (n + 1) * columns] = total
        rounded[:, n * columns : (n + 1) * columns] = total.astype(rounded.dtype)


def gate_up_sums(values, own, other):
    chips, width, rows = values.shape
    columns = 2 * own.shape[2]
    return pl.pallas_call(
        gate_up_kernel,
        out_shape=(
            jax.ShapeDtypeStruct((rows, columns), jnp.float32),
            jax.ShapeDtypeStruct((rows, columns), jnp.bfloat16),
        ),
        in_specs=whole(3),
        out_specs=tuple(whole(2)),
        compiler_params=pltpu.CompilerParams(vmem_limit_bytes=24 << 20),
        cost_estimate=pl.CostEstimate(
            flops=2 * chips * rows * width * columns,
            bytes_accessed=4 * own.size + 2 * values.size + 6 * rows * columns,
            transcendentals=0,
        ),
    )(values, own, other)


def down_kernel(sums, partner, own, other, out):
    units = own.shape[2]
    total = sums[...] + partner[...].astype(jnp.float32)
    values = []
    for n in range(2):
        gate = total[:, 2 * n * units : (2 * n + 1) * units]
        up = total[:, (2 * n + 1) * units : (2 * n + 2) * units]
        values.append((jax.nn.silu(gate) * up).astype(jnp.bfloat16))
    for i in range(out.shape[0]):
        mixed = lax.dot_general(own[i], values[0], MINOR, preferred_element_type=jnp.float32)
        mixed += lax.dot_general(other[i], values[1], MINOR, preferred_element_type=jnp.float32)
        out[i] = mixed.astype(out.dtype)


def down_sums(sums, partner, own, other):
    chips, width, units = own.shape
    rows = sums.shape[0]
    return pl.pallas_call(
        down_kernel,
        out_shape=jax.ShapeDtypeStruct((chips, width, rows), jnp.bfloat16),
        in_specs=whole(4),
        out_specs=pl.BlockSpec(memory_space=pltpu.VMEM),
        compiler_params=pltpu.CompilerParams(vmem_limit_bytes=24 << 20),
        cost_estimate=pl.CostEstimate(
            flops=4 * chips * rows * width * units,
            bytes_accessed=4 * own.size + 6 * sums.size + 2 * chips * rows * width,
            transcendentals=2 * rows * units,
        ),
    )(sums, partner, own, other)


def whole(count):
    return [pl.BlockSpec(memory_space=pltpu.VMEM)] * count


def page_kernel(moves, first, rest, lower, higher):
    lower[...] = first[...]
    higher[...] = rest[...]


def departing_pages(latent_pool, page_moves):
    block = (1,) + latent_pool.shape[1:]
    moving = page_moves.shape[1] // 2
    shape = jax.ShapeDtypeStruct((moving,) + latent_pool.shape[1:], latent_pool.dtype)
    return pl.pallas_call(
        page_kernel,
        out_shape=(shape, shape),
        grid_spec=pltpu.PrefetchScalarGridSpec(
            num_scalar_prefetch=1,
            grid=(moving,),
            in_specs=[
                pl.BlockSpec(block, lambda i, moves: (moves[0, i], 0, 0)),
                pl.BlockSpec(block, lambda i, moves: (moves[0, moving + i], 0, 0)),
            ],
            out_specs=[pl.BlockSpec(block, lambda i, moves: (i, 0, 0))] * 2,
        ),
        cost_estimate=pl.CostEstimate(
            flops=0, bytes_accessed=8 * moving * block[1] * block[2], transcendentals=0
        ),
    )(page_moves, latent_pool, latent_pool)


def attention_kernel(page_list, lengths, queries, pool, low, high, out, rows):
    count, page = page_list.shape[1], pool.shape[1]
    moving = low.shape[0]
    for j in range(count):
        number = page_list[0, j]
        if j < 2 * moving:
            number = number - pool.shape[0]
            upper = number >= moving
            from_low = low[jnp.where(upper, 0, number)]
            from_high = high[jnp.where(upper, number - moving, 0)]
            block = jnp.where(upper, from_high, from_low)
        else:
            block = pool[number]
        rows[j * page : (j + 1) * page, :] = block
    scores = lax.dot_general(
        queries[0], rows[...], (((1,), (1,)), ((), ())), preferred_element_type=jnp.float32
    )
    place = lax.broadcasted_iota(jnp.int32, scores.shape, 1)
    scores = jnp.where(place < lengths[0], scores * softmax_scale, -1e30)
    values = jnp.exp(scores - jnp.max(scores, axis=1, keepdims=True))
    weights = (values / jnp.sum(values, axis=1, keepdims=True)).astype(jnp.bfloat16)
    mixed = jnp.dot(weights, rows[:, : out.shape[2]], preferred_element_type=jnp.float32)
    out[0] = mixed.astype(out.dtype)


def attention(queries, latent_pool, low, high, page_list, lengths):
    _, heads, width = queries.shape
    count = page_list.shape[1] * latent_pool.shape[1]
    return pl.pallas_call(
        attention_kernel,
        out_shape=jax.ShapeDtypeStruct((1, heads, KVL), jnp.bfloat16),
        in_specs=[pl.BlockSpec(memory_space=pltpu.SMEM)] * 2 + whole(4),
        out_specs=pl.BlockSpec(memory_space=pltpu.VMEM),
        scratch_shapes=[pltpu.VMEM((count, width), jnp.bfloat16)],
        compiler_params=pltpu.CompilerParams(vmem_limit_bytes=16 << 20),
        cost_estimate=pl.CostEstimate(
            flops=2 * heads * count * (width + KVL),
            bytes_accessed=2 * (latent_pool.size + 2 * queries.size),
            transcendentals=heads * count,
        ),
    )(page_list, lengths, queries, latent_pool, low, high)


def prepare_kernel(tokens, chosen, affinity, out):
    chips, lines, lanes = out.shape[0] // 2, out.shape[1], out.shape[2]
    row = tokens[...].astype(jnp.float32)
    width = row.shape[1] // chips
    choices = chosen.shape[2]
    routing = [chosen[0].astype(jnp.float32), affinity[0].astype(jnp.float32)]
    routing.append(jnp.zeros((1, lines * lanes - width - 2 * choices), jnp.float32))
    for p in range(chips):
        start = p * width
        block = [row[:, start + n * lanes : start + (n + 1) * lanes] for n in range(lines - 1)]
        last = [row[:, start + (lines - 1) * lanes : start + width]] + routing
        block.append(jnp.concatenate(last, axis=1))
        block = jnp.concatenate(block, axis=0).astype(out.dtype)
        out[2 * p] = block
        out[2 * p + 1] = block


def prepared(tokens, expert_ids, affinity, members):
    return pl.pallas_call(
        prepare_kernel,
        out_shape=jax.ShapeDtypeStruct((members, 4, 128), jnp.bfloat16),
        in_specs=whole(3),
        out_specs=pl.BlockSpec(memory_space=pltpu.VMEM),
        cost_estimate=pl.CostEstimate(
            flops=0, bytes_accessed=4 * tokens.size, transcendentals=0
        ),
    )(tokens, expert_ids, affinity)


def sum_kernel(parts, out):
    sums = parts[0].astype(jnp.float32)
    for n in range(1, parts.shape[0]):
        sums += parts[n].astype(jnp.float32)
    sums = sums.T
    half = sums.shape[0] // 2
    sums = jnp.concatenate([sums[:half], sums[half:]], axis=1)
    out[...] = sums.reshape(out.shape).astype(out.dtype)


def added(parts, groups):
    _, width, rows = parts.shape
    return pl.pallas_call(
        sum_kernel,
        out_shape=jax.ShapeDtypeStruct((groups, rows // groups // 2, 2 * width), jnp.bfloat16),
        in_specs=whole(1),
        out_specs=pl.BlockSpec(memory_space=pltpu.VMEM),
        compiler_params=pltpu.CompilerParams(vmem_limit_bytes=24 << 20),
        cost_estimate=pl.CostEstimate(
            flops=parts.size, bytes_accessed=2 * parts.size, transcendentals=0
        ),
    )(parts)


def shards(
    tokens,
    expert_ids,
    affinity,
    gate_up_blocks,
    down_blocks,
    queries,
    latent_pool,
    page_moves,
    page_list,
    lengths,
):
    members = lax.axis_size(EP)
    groups = lax.axis_size("z")
    chips = members // 4
    choices = expert_ids.shape[2]
    slots = members * choices // groups // 2
    rows = groups * slots
    units = gate_up_blocks.shape[3] // 2
    width = 2 * tokens.shape[1] // members
    between_cores = [(0, 1), (1, 0)]
    held = exchanged(prepared(tokens, expert_ids, affinity, members), EP)
    gate_up = gate_up_blocks.reshape(chips, width, 2 * units)
    other_gate_up = lax.ppermute(gate_up, "c", between_cores)
    other_down = lax.ppermute(down_blocks, "c", between_cores)
    held, page_moves, other_gate_up, down_blocks, other_down = lax.optimization_barrier(
        (held, page_moves, other_gate_up, down_blocks, other_down)
    )
    held = held.reshape(members, -1)
    chosen = held[:, width : width + choices].astype(jnp.float32)
    affinity_all = held[:, width + choices : width + 2 * choices].astype(jnp.float32)
    route_weights = routed_scale * affinity_all / jnp.sum(affinity_all, axis=1, keepdims=True)
    matches = chosen[:, :, None] == jnp.arange(groups, dtype=jnp.float32)[None, None, :]
    member = jnp.any(matches, axis=1)
    weight_of = jnp.sum(jnp.where(matches, route_weights[:, :, None], 0.0), axis=1)
    earlier = jnp.arange(members)[:, None] > jnp.arange(members)[None, :]
    position = jnp.dot(
        earlier.astype(jnp.bfloat16),
        member.astype(jnp.bfloat16),
        preferred_element_type=jnp.float32,
    )
    slot_number = (jnp.arange(slots) + lax.axis_index("c") * slots).astype(jnp.float32)
    selector = member.T[:, None, :] & (position.T[:, None, :] == slot_number[None, :, None])
    selector = selector.reshape(groups, slots // 2, 2, members)
    sides = [selector[:, :, n].reshape(rows // 2, members) for n in range(2)]
    sent_rows = jnp.concatenate(
        [
            jnp.dot(
                side.astype(jnp.bfloat16), held[:, :width], preferred_element_type=jnp.float32
            ).astype(jnp.bfloat16)
            for side in sides
        ],
        axis=1,
    )
    paired = (groups, slots // 2, 2 * width)
    arrived = exchanged(sent_rows.reshape(paired), "z").reshape(rows // 2, 2 * width)
    to_lower, to_higher = departing_pages(latent_pool, page_moves)
    forward = [(i, (i + 1) % members) for i in range(members)]
    backward = [(target, source) for source, target in forward]
    low = lax.ppermute(to_higher, EP, forward)
    high = lax.ppermute(to_lower, EP, backward)
    down = down_blocks.reshape(units, chips, width).transpose(1, 2, 0)
    other_down = other_down.reshape(units, chips, width).transpose(1, 2, 0)
    arrived, low, high, down, other_down = lax.optimization_barrier(
        (arrived, low, high, down, other_down)
    )
    arrived = jnp.concatenate([arrived[:, :width].T, arrived[:, width:].T], axis=1)
    gathered = exchanged(jnp.broadcast_to(arrived[None], (chips, width, rows)), ("y", "x"))
    sums, rounded = gate_up_sums(gathered, gate_up, other_gate_up)
    partner = lax.ppermute(rounded, "h", [(0, 1), (1, 0)])
    block_sums = down_sums(sums, partner, down, other_down)
    summed = added(exchanged(block_sums, ("y", "x")), groups)
    summed, low, high = lax.optimization_barrier((summed, low, high))
    attention_latent = attention(queries, latent_pool, low, high, page_list, lengths)
    returned = exchanged(summed, "z").reshape(rows // 2, 2 * width)
    returned, attention_latent = lax.optimization_barrier((returned, attention_latent))
    weight_rows = weight_of.T[:, None, :]
    mixed = jnp.zeros((members, width), jnp.float32)
    for n in range(2):
        weighted = jnp.where(selector[:, :, n], weight_rows, 0.0).reshape(rows // 2, members)
        values = returned[:, n * width : (n + 1) * width].astype(jnp.float32)
        mixed += jnp.einsum("rn,rk->nk", weighted, values, precision=lax.Precision.HIGHEST)
    mixed = mixed.astype(jnp.bfloat16).reshape(members, 2, width // 2)
    halves = exchanged(mixed, EP).reshape(members // 2, 2, width)
    expert_mix = jnp.sum(halves.astype(jnp.float32), axis=1).astype(jnp.bfloat16).reshape(1, -1)
    return (attention_latent, expert_mix)


def solution(mesh):
    fine = Mesh(mesh.devices.reshape(32, 2, 2, 4, 2), ("z",) + EP)
    both = ("z",) + EP
    placed = (
        P(both, None),
        P("z", EP, None),
        P("z", EP, None),
        P("z", EP, None, None),
        P("z", EP, None, None),
        P(both, None, None),
        P(both, None, None),
        P(both, None),
        P(both, None),
        P(both),
    )
    return jax.shard_map(
        shards,
        mesh=fine,
        in_specs=placed,
        out_specs=(P(both, None, None), P(both, None)),
        check_vma=False,
    )
```
